32 devices in a mesh: gx: 8 (over y, x, core), gy: 4 (over z).
Axes of the slice: x: 2, y: 2, z: 4, core: 2. Of those that a mesh axis runs over, the one named last changes fastest.
Arguments:
- velocity: float32 [3, 64, 128, 128], P(None, 'gx', 'gy'), may hold values from -6 to 6
- forcing: float32 [3, 64, 128, 128], P(None, 'gx', 'gy'), may hold values from -6 to 6
- viscosity: float32 [64, 128, 128], P('gx', 'gy'), may hold values from 0.1 to 2
- multipliers: float32 [8, 4, 8, 3, 384], P('gx', 'gy'), may hold values from -4 to 4
- sphere_centres: int32 [8, 4, 8, 3], P('gx', 'gy'), may hold values from 0 to 119, as said below
- sphere_offsets: int32 [8, 4, 8, 3, 384], P('gx', 'gy'), may hold values from -8 to 8, as said below
- sphere_count: int32 [8, 4], P('gx', 'gy'), may hold values from 1 to 8, as said below
Outputs:
- velocity_out: float32 [3, 64, 128, 128], P(None, 'gx', 'gy')
- body_motion: float32 [8, 4, 8, 6], P('gx', 'gy')
The draws below stay inside these ranges and needn't reach their ends.
Inputs may be any that keep to these rules, and one draw needn't show every extreme that they name: `sphere_centres`: the first two coordinates of a slot's centre lie in its owner's block, 0 to 7 and 0 to 31, the third lies in 8 to 119; some slot reaches each end. `sphere_offsets`: every point lies at a distance between 7 and 8 from its sphere's centre. Slots 0 to sphere_count - 1 of a device hold spheres, the others are empty; in every draw some device fills all 8 slots and some device has one sphere.
All inputs are finite; a program needn't handle non-finite values.
Results may differ from the reference program's by a relative error of at most 0.0001.
Values sent between devices are 32-bit elements; how exact they have to be, the bound alone decides.
A program may use at most 128 MiB of HBM per device.

```python
import math
import jax
import jax.numpy as jnp
from jax import lax

CX = 8
CY = 32
NZ = 128
RAD = 8
SLOTS = 8
M = 384
SWEEPS = 4
UZ = 3
NX = 64
NY = 128
N_GX = 8
N_GY = 4


def draw_sphere_centres(key, part):
    rows_x = NX // CX
    rows_y = NY // CY
    subkeys = jax.random.split(key, 5)
    slot_shape = (rows_x, rows_y, SLOTS)
    cell_x = jax.random.randint(subkeys[0], slot_shape, 0, CX)
    cell_y = jax.random.randint(subkeys[1], slot_shape, 0, CY)
    cell_z = jax.random.randint(subkeys[2], slot_shape, RAD, NZ - RAD)
    top_slot = jax.random.randint(subkeys[3], (rows_x, rows_y, 1), 0, SLOTS)
    low_slot = jax.random.randint(subkeys[4], (rows_x, rows_y, 1), 0, SLOTS)
    slot_index = jnp.arange(SLOTS)[None, None, :]
    at_top = slot_index == top_slot
    at_low = (slot_index == low_slot) & jnp.logical_not(at_top)
    cell_x = jnp.where(at_top, CX - 1, jnp.where(at_low, 0, cell_x))
    cell_y = jnp.where(at_top, CY - 1, jnp.where(at_low, 0, cell_y))
    cell_z = jnp.where(at_top, NZ - RAD - 1, jnp.where(at_low, RAD, cell_z))
    return jnp.stack([cell_x, cell_y, cell_z], -1).astype(jnp.int32)


def integer_root(remaining):
    steps = jnp.arange(1, RAD + 1).astype(jnp.int32)
    return jnp.sum((steps * steps <= remaining[..., None]).astype(jnp.int32), -1).astype(jnp.int32)


def draw_sphere_offsets(key, part):
    rows_x = NX // CX
    rows_y = NY // CY
    subkeys = jax.random.split(key, 4)
    point_shape = (rows_x, rows_y, SLOTS, M)
    first = jax.random.randint(subkeys[0], point_shape, -RAD, RAD + 1)
    reach = integer_root(RAD * RAD - first * first)
    second = jax.random.randint(subkeys[1], point_shape, -reach, reach + 1)
    third_size = integer_root(RAD * RAD - first * first - second * second)
    signs = jax.random.randint(subkeys[2], point_shape, 0, 2) * 2 - 1
    third = signs * third_size
    triple = jnp.stack([first, second, third], -1)
    rotate = jax.random.randint(subkeys[3], point_shape, 0, 3)
    order = (jnp.arange(3)[None, None, None, None, :] + rotate[..., None]) % 3
    placed = jnp.take_along_axis(triple, order, axis=-1)
    return jnp.moveaxis(placed, -1, 3).astype(jnp.int32)


def draw_sphere_count(key, part):
    rows_x = NX // CX
    rows_y = NY // CY
    subkeys = jax.random.split(key, 4)
    base_count = jax.random.randint(subkeys[0], (rows_x, rows_y), 1, SLOTS // 2 + 1)
    doubled = jax.random.randint(subkeys[1], (rows_x, rows_y), 0, 4) == 0
    counts = jnp.where(doubled, 2 * base_count, base_count)
    device_index = jnp.arange(rows_x * rows_y).reshape(rows_x, rows_y)
    full_device = jax.random.randint(subkeys[2], (), 0, rows_x * rows_y)
    single_device = jax.random.randint(subkeys[3], (), 0, rows_x * rows_y)
    counts = jnp.where(device_index == full_device, SLOTS, jnp.where(device_index == single_device, 1, counts))
    return counts.astype(jnp.int32)


def block_scale(key, extent, cuts, least, top_value):
    factor_of, own = 1.0, jax.random.fold_in(key, 6)
    for position, parts in cuts:
        heights = jnp.exp(jax.random.uniform(jax.random.fold_in(own, position), (parts,), jnp.float32, least / len(cuts), top_value / len(cuts)))
        factor_of = factor_of * jnp.repeat(heights, extent[position] // parts).reshape([-1 if axis == position else 1 for axis in range(len(extent))])
    return factor_of


def gaussian(stream_key, dims, deviation, bound, cuts=(), kind=jnp.bfloat16):
    entries = jax.random.normal(stream_key, dims, jnp.float32) * deviation
    if len(cuts) > 0:
        entries = block_scale(stream_key, dims, cuts, -0.22, 0.18) * entries
    return jnp.clip(entries, min=-bound, max=bound).astype(kind)


def setup_inputs(seed: int = 0) -> dict:
    key_of = jax.random.split(jax.random.key(seed), 8)
    velocity = gaussian(key_of[0], (3, NX, NY, NZ), 1.0, 6.0, ((1, 8), (2, 4)), jnp.float32)
    forcing = gaussian(key_of[1], (3, NX, NY, NZ), 1.0, 6.0, ((1, 8), (2, 4)), jnp.float32)
    viscosity = jnp.clip(jnp.exp(math.log(2.0) - 2.9957323 * jax.random.uniform(key_of[2], (NX, NY, NZ), jnp.float32) ** block_scale(key_of[2], (NX, NY, NZ), ((0, 8), (1, 4)), -0.2, 0.2)), 0.1, 2.0)
    multipliers = gaussian(key_of[3], (N_GX, N_GY, SLOTS, 3, M), 0.5, 4.0, ((0, 8), (1, 4)), jnp.float32)
    sphere_centres = draw_sphere_centres(jax.random.fold_in(key_of[7], 71), 0)
    sphere_offsets = draw_sphere_offsets(jax.random.fold_in(key_of[7], 71), 0)
    sphere_count = draw_sphere_count(jax.random.fold_in(key_of[7], 71), 0)
    return {"velocity": velocity, "forcing": forcing, "viscosity": viscosity, "multipliers": multipliers, "sphere_centres": sphere_centres, "sphere_offsets": sphere_offsets, "sphere_count": sphere_count}


MASS_TERM = 0.2
VERTICAL_WEIGHT = 0.25
UZAWA_STEP = 0.5


def cross_product(left, right):
    return jnp.stack([left[..., 1, :] * right[..., 2, :] - left[..., 2, :] * right[..., 1, :],
                      left[..., 2, :] * right[..., 0, :] - left[..., 0, :] * right[..., 2, :],
                      left[..., 0, :] * right[..., 1, :] - left[..., 1, :] * right[..., 0, :]], -2)


def face_terms(viscous):
    centre = viscous[1:-1, 1:-1, :]
    vertical = jnp.concatenate([viscous[:, :, :1], viscous, viscous[:, :, -1:]], axis=2)
    k_west = 0.5 * (centre + viscous[:-2, 1:-1, :])
    k_east = 0.5 * (centre + viscous[2:, 1:-1, :])
    k_south = 0.5 * (centre + viscous[1:-1, :-2, :])
    k_north = 0.5 * (centre + viscous[1:-1, 2:, :])
    k_below = VERTICAL_WEIGHT * 0.5 * (centre + vertical[1:-1, 1:-1, :-2])
    k_above = VERTICAL_WEIGHT * 0.5 * (centre + vertical[1:-1, 1:-1, 2:])
    inverse = 1.0 / (MASS_TERM + k_west + k_east + k_south + k_north + k_below + k_above)
    return (k_west, k_east, k_south, k_north, k_below, k_above, inverse)


def jacobi_step(padded, terms, source):
    k_west, k_east, k_south, k_north, k_below, k_above, inverse = terms
    interior = padded[..., 1:-1, 1:-1, :]
    zero_plane = jnp.zeros(interior.shape[:-1] + (1,), interior.dtype)
    column_pad = jnp.concatenate([zero_plane, interior, zero_plane], axis=-1)
    numerator = (source + k_west * padded[..., :-2, 1:-1, :] + k_east * padded[..., 2:, 1:-1, :]
                 + k_south * padded[..., 1:-1, :-2, :] + k_north * padded[..., 1:-1, 2:, :]
                 + k_below * column_pad[..., :-2] + k_above * column_pad[..., 2:])
    return numerator * inverse


def relax_global(flow, terms, source):
    def one_component(operands):
        current, right_side = operands
        for sweep_index in range(SWEEPS):
            padded = jnp.pad(current, ((1, 1), (1, 1), (0, 0)), mode="wrap")
            current = jacobi_step(padded, terms, right_side)
        return current

    return lax.map(one_component, (flow, source))


def reference(velocity, forcing, viscosity, multipliers, sphere_centres, sphere_offsets, sphere_count):
    live = (jnp.arange(SLOTS)[None, None, :] < sphere_count[:, :, None]).astype(jnp.float32)
    anchor_x = (jnp.arange(N_GX) * CX).astype(jnp.int32)[:, None, None, None]
    anchor_y = (jnp.arange(N_GY) * CY).astype(jnp.int32)[None, :, None, None]
    cell_x = (anchor_x + sphere_centres[..., 0:1] + sphere_offsets[..., 0, :]) % NX
    cell_y = (anchor_y + sphere_centres[..., 1:2] + sphere_offsets[..., 1, :]) % NY
    cell_z = sphere_centres[..., 2:3] + sphere_offsets[..., 2, :]
    flat_cells = ((cell_x * NY + cell_y) * NZ + cell_z).reshape(-1).astype(jnp.int32)
    radius = sphere_offsets.astype(jnp.float32)
    spread_sum = jnp.sum(radius * radius, axis=(3, 4))
    terms = face_terms(jnp.pad(viscosity, ((1, 1), (1, 1), (0, 0)), mode="wrap"))
    multiplier = multipliers
    flow = velocity
    mean_velocity = None
    spin = None
    for round_index in range(UZ):
        weighted = multiplier * live[..., None, None]
        spread_values = jnp.moveaxis(weighted, 3, 0).reshape(3, -1)
        force = jnp.zeros((3, NX * NY * NZ), jnp.float32).at[:, flat_cells].add(spread_values)
        flow = relax_global(flow, terms, forcing + force.reshape(3, NX, NY, NZ))
        sampled = flow.reshape(3, -1)[:, flat_cells].reshape(3, N_GX, N_GY, SLOTS, M)
        sampled = jnp.moveaxis(sampled, 0, 3) * live[..., None, None]
        mean_velocity = jnp.sum(sampled, -1) / M
        moment = jnp.sum(cross_product(radius, sampled), -1)
        spin = 1.5 * moment / spread_sum[..., None]
        if round_index + 1 < UZ:
            target = mean_velocity[..., None] + cross_product(spin[..., None], radius)
            multiplier = multiplier + UZAWA_STEP * (target - sampled)
    motion = jnp.concatenate([mean_velocity, spin], -1)
    return flow, motion
```

```python
import functools

import jax
import jax.numpy as jnp
from jax import lax
from jax.experimental import pallas as pl
from jax.experimental.pallas import tpu as pltpu
from jax.sharding import PartitionSpec as P

SWEEPS = 4
UZ = 3
REACH = 8
WINDOW = 24

MASS_TERM = 0.2
VERTICAL_WEIGHT = 0.25
UZAWA_STEP = 0.5

MESH = pl.DeviceIdType.MESH
VM = pl.BlockSpec(memory_space=pltpu.VMEM)
SM = pl.BlockSpec(memory_space=pltpu.SMEM)
F32 = jnp.float32
BF16 = jnp.bfloat16


def around():
    nx, ny = lax.axis_size("gx"), lax.axis_size("gy")
    me_x, me_y = lax.axis_index("gx"), lax.axis_index("gy")
    left = (lax.rem(me_x + nx - 1, nx), me_y)
    right = (lax.rem(me_x + 1, nx), me_y)
    down = (me_x, lax.rem(me_y + ny - 1, ny))
    up = (me_x, lax.rem(me_y + 1, ny))
    return left, right, down, up


def greet(devices):
    barrier = pltpu.get_barrier_semaphore()
    for device in devices:
        pl.semaphore_signal(barrier, inc=1, device_id=device, device_id_type=MESH)
    pl.semaphore_wait(barrier, len(devices))


def send(src, dst, sems, index, device):
    copy = pltpu.make_async_remote_copy(
        src_ref=src,
        dst_ref=dst,
        send_sem=sems.at[0, index],
        recv_sem=sems.at[1, index],
        device_id=device,
        device_id_type=MESH,
    )
    copy.start()
    return copy


def scatter_kernel(meta, key, depth, lam, out):
    width_x = out.shape[1]
    height = out.shape[3]
    rows = width_x * WINDOW
    slots, points = key.shape
    out[...] = jnp.zeros_like(out)

    def one(s, carry):
        @pl.when(meta[1, s] > 0)
        def _():
            base = pl.multiple_of(meta[0, s], 8)
            row_key = key[pl.ds(s, 1), :]
            row_z = depth[pl.ds(s, 1), :]
            mask = lax.broadcasted_iota(jnp.int32, (rows, points), 0) == row_key
            mask = jnp.where(mask, 1.0, 0.0).astype(BF16)
            at_z = lax.broadcasted_iota(jnp.int32, (height, points), 0) == row_z
            high, low = [], []
            for c in range(3):
                value = lam[c, pl.ds(s, 1), :]
                top = value.astype(BF16).astype(F32)
                high.append(jnp.where(at_z, top, 0.0).astype(BF16))
                low.append(jnp.where(at_z, value - top, 0.0).astype(BF16))
            dims = (((1,), (1,)), ((), ()))
            got = lax.dot_general(
                mask, jnp.concatenate(high, 0), dims, preferred_element_type=F32
            ) + lax.dot_general(
                mask, jnp.concatenate(low, 0), dims, preferred_element_type=F32
            )
            for c in range(3):
                part = got[:, c * height:(c + 1) * height].reshape(width_x, WINDOW, height)
                out[c, :, pl.ds(base, WINDOW), :] += part

        return carry

    lax.fori_loop(0, slots, one, 0)


def gather_kernel(meta, key, depth, field, out):
    width_x = field.shape[1]
    height = field.shape[3]
    rows = width_x * WINDOW
    slots, points = key.shape
    out[...] = jnp.zeros_like(out)

    def one(s, carry):
        @pl.when(meta[1, s] > 0)
        def _():
            base = pl.multiple_of(meta[0, s], 8)
            row_key = key[pl.ds(s, 1), :]
            row_z = depth[pl.ds(s, 1), :]
            mask = lax.broadcasted_iota(jnp.int32, (rows, points), 0) == row_key
            at_z = lax.broadcasted_iota(jnp.int32, (height, points), 0) == row_z
            at_z = jnp.where(at_z, 1.0, 0.0).astype(BF16)
            at_z = jnp.concatenate([at_z, at_z], 0)
            for c in range(3):
                value = field[c, :, pl.ds(base, WINDOW), :].reshape(rows, height)
                top = value.astype(BF16)
                rest = (value - top.astype(F32)).astype(BF16)
                got = jnp.dot(
                    jnp.concatenate([top, rest], 1), at_z, preferred_element_type=F32
                )
                out[c, pl.ds(s, 1), :] = jnp.sum(
                    jnp.where(mask, got, 0.0), axis=0, keepdims=True
                )

        return carry

    lax.fori_loop(0, slots, one, 0)


def relax_kernel(
    flow, forcing, partial, terms, out, work, source, xh, ys, yh, ph, gh, xsem, ysem, psem, gsem
):
    left, right, down, up = around()
    width_x, width_y, height = flow.shape[1:]
    lo, hi = REACH, REACH + width_y
    greet((left, right, down, up))
    share = [
        send(partial.at[:, :, pl.ds(0, REACH), :], ph.at[1], psem, 1, down),
        send(partial.at[:, :, pl.ds(hi, REACH), :], ph.at[0], psem, 0, up),
    ]
    sends = []

    def exchange(step, x_ref, first_row, last_row):
        for c in range(3):
            ys[step, 1, c] = x_ref[c, :, first_row, :]
            ys[step, 0, c] = x_ref[c, :, last_row, :]
        rows = pl.ds(first_row, width_y)
        return [
            send(x_ref.at[:, 0, rows, :], xh.at[step, 1], xsem.at[step], 1, left),
            send(x_ref.at[:, width_x - 1, rows, :], xh.at[step, 0], xsem.at[step], 0, right),
            send(ys.at[step, 1], yh.at[step, 1], ysem.at[step], 1, down),
            send(ys.at[step, 0], yh.at[step, 0], ysem.at[step], 0, up),
        ]

    sends = exchange(0, flow, 0, width_y - 1)
    work[0, :, :, lo:hi, :] = flow[...]
    for copy in share:
        copy.wait()
    source[...] = forcing[...] + partial[:, :, lo:hi, :]
    source[:, :, 0:REACH, :] += ph[0]
    source[:, :, width_y - REACH:width_y, :] += ph[1]
    source[...] = source[...] * terms[6][None]

    for step in range(SWEEPS):
        for copy in sends:
            copy.wait()
        for c in range(3):
            for i in range(width_x):
                work[step, c, i, lo - 1:lo, :] = yh[step, 0, c, i:i + 1, :]
                work[step, c, i, hi:hi + 1, :] = yh[step, 1, c, i:i + 1, :]
        target = work.at[step + 1] if step + 1 < SWEEPS else out

        def component(c, carry):
            for i in range(width_x):
                here = work[step, c, i, lo:hi, :]
                west = xh[step, 0, c] if i == 0 else work[step, c, i - 1, lo:hi, :]
                east = xh[step, 1, c] if i == width_x - 1 else work[step, c, i + 1, lo:hi, :]
                south = work[step, c, i, lo - 1:hi - 1, :]
                north = work[step, c, i, lo + 1:hi + 1, :]
                target[c, i, lo:hi, :] = (
                    source[c, i]
                    + terms[0, i] * west
                    + terms[1, i] * east
                    + terms[2, i] * south
                    + terms[3, i] * north
                    + terms[4, i] * pltpu.roll(here, 1, 1)
                    + terms[5, i] * pltpu.roll(here, height - 1, 1)
                )
            return carry

        lax.fori_loop(0, 3, component, 0)
        if step + 1 < SWEEPS:
            sends = exchange(step + 1, target, lo, hi - 1)

    last = [
        send(out.at[:, :, pl.ds(lo, REACH), :], gh.at[1], gsem, 1, down),
        send(out.at[:, :, pl.ds(hi - REACH, REACH), :], gh.at[0], gsem, 0, up),
    ]
    for copy in last:
        copy.wait()
    out[:, :, 0:lo, :] = gh[0]
    out[:, :, hi:hi + REACH, :] = gh[1]


def body_kernel(final, sampled, radius, lam, out, motion, wh, lh, new, wsem, lsem):
    left, right, _, _ = around()
    slots, points = radius.shape[1:]
    greet((left, right))
    sends = [
        send(sampled.at[:, pl.ds(0, slots), :], wh.at[1], wsem, 1, left),
        send(sampled.at[:, pl.ds(2 * slots, slots), :], wh.at[0], wsem, 0, right),
    ]
    r = [radius[c] for c in range(3)]
    spread = jnp.sum(r[0] * r[0] + r[1] * r[1] + r[2] * r[2], axis=1, keepdims=True)
    for copy in sends:
        copy.wait()
    w = [sampled[c, slots:2 * slots, :] + wh[0, c] + wh[1, c] for c in range(3)]
    mean = [jnp.sum(w[c], axis=1, keepdims=True) / points for c in range(3)]
    spin = []
    for c in range(3):
        a, b = (c + 1) % 3, (c + 2) % 3
        moment = jnp.sum(r[a] * w[b] - r[b] * w[a], axis=1, keepdims=True)
        spin.append(1.5 * moment / spread)
    lane = lax.broadcasted_iota(jnp.int32, motion.shape, 1)
    row = jnp.zeros(motion.shape, F32)
    for c, value in enumerate(mean + spin):
        row = jnp.where(lane == c, value, row)
    motion[...] = row
    if final:
        out[...] = jnp.zeros_like(out)
        return
    for c in range(3):
        a, b = (c + 1) % 3, (c + 2) % 3
        target = mean[c] + (spin[a] * r[b] - spin[b] * r[a])
        new[c] = lam[c, slots:2 * slots, :] + UZAWA_STEP * (target - w[c])
    sends = [
        send(new, lh.at[1], lsem, 1, left),
        send(new, lh.at[0], lsem, 0, right),
    ]
    out[:, slots:2 * slots, :] = new[...]
    for copy in sends:
        copy.wait()
    out[:, 0:slots, :] = lh[0]
    out[:, 2 * slots:3 * slots, :] = lh[1]


def pair(block, axis, dim, width):
    count = lax.axis_size(axis)
    forward = [(i, (i + 1) % count) for i in range(count)]
    backward = [(target, source) for source, target in forward]
    size = block.shape[dim]
    low = lax.ppermute(lax.slice_in_dim(block, size - width, size, axis=dim), axis, forward)
    high = lax.ppermute(lax.slice_in_dim(block, 0, width, axis=dim), axis, backward)
    return jnp.concatenate([low, block, high], axis=dim)


def face_terms(nu):
    along_x = pair(nu, "gx", 0, 1)
    along_y = pair(nu, "gy", 1, 1)
    along_z = jnp.concatenate([nu[:, :, :1], nu, nu[:, :, -1:]], axis=2)
    k = [
        0.5 * (nu + along_x[:-2]),
        0.5 * (nu + along_x[2:]),
        0.5 * (nu + along_y[:, :-2]),
        0.5 * (nu + along_y[:, 2:]),
        VERTICAL_WEIGHT * 0.5 * (nu + along_z[:, :, :-2]),
        VERTICAL_WEIGHT * 0.5 * (nu + along_z[:, :, 2:]),
    ]
    inverse = 1.0 / (MASS_TERM + k[0] + k[1] + k[2] + k[3] + k[4] + k[5])
    z = jnp.arange(nu.shape[2])
    k[4] = jnp.where(z == 0, 0.0, k[4])
    k[5] = jnp.where(z == nu.shape[2] - 1, 0.0, k[5])
    return jnp.stack([face * inverse for face in k] + [inverse])


def on_device(
    velocity, forcing, viscosity, multipliers, sphere_centres, sphere_offsets, sphere_count
):
    _, width_x, width_y, height = velocity.shape
    slots, points = multipliers.shape[2], multipliers.shape[4]
    live = jnp.arange(slots) < sphere_count[0, 0]
    centres = sphere_centres[0, 0]
    offsets = jnp.moveaxis(sphere_offsets[0, 0], 1, 0)
    base = (centres[:, 1] // 8) * 8
    own_x = jnp.where(live[:, None], centres[:, 0:1] + offsets[0], -8 * width_x)
    own_y = (centres[:, 1] - base)[:, None] + offsets[1] + REACH
    own_z = centres[:, 2:3] + offsets[2]
    geometry = jnp.stack(
        [own_x, own_y, own_z, jnp.broadcast_to(base[:, None], own_x.shape)]
    ).astype(jnp.int32)
    near = pair(geometry, "gx", 1, slots)
    shift = jnp.repeat((jnp.arange(3) - 1) * width_x, slots)[:, None]
    local_x = near[0] + shift
    inside = (local_x >= 0) & (local_x < width_x)
    key = jnp.where(inside, local_x * WINDOW + near[1], -1).astype(jnp.int32)
    depth = near[2]
    meta = jnp.stack([near[3, :, 0], jnp.any(inside, 1).astype(jnp.int32)])
    radius = offsets.astype(F32)
    lam = pair(jnp.moveaxis(multipliers[0, 0], 1, 0), "gx", 1, slots)
    terms = face_terms(viscosity)

    wide = (3, width_x, width_y + 2 * REACH, height)
    shape = jax.ShapeDtypeStruct
    limit = 48 * 1024 * 1024
    scatter = pl.pallas_call(
        scatter_kernel,
        name="spread_force",
        out_shape=shape(wide, F32),
        in_specs=[SM, VM, VM, VM],
        out_specs=VM,
        compiler_params=pltpu.CompilerParams(vmem_limit_bytes=limit),
    )
    gather = pl.pallas_call(
        gather_kernel,
        name="sample_flow",
        out_shape=shape((3, 3 * slots, points), F32),
        in_specs=[SM, VM, VM, VM],
        out_specs=VM,
        compiler_params=pltpu.CompilerParams(vmem_limit_bytes=limit),
    )
    relax = pl.pallas_call(
        relax_kernel,
        name="relax_flow",
        out_shape=shape(wide, F32),
        in_specs=[VM] * 4,
        out_specs=VM,
        scratch_shapes=[
            pltpu.VMEM((SWEEPS,) + wide, F32),
            pltpu.VMEM((3, width_x, width_y, height), F32),
            pltpu.VMEM((SWEEPS, 2, 3, width_y, height), F32),
            pltpu.VMEM((SWEEPS, 2, 3, width_x, height), F32),
            pltpu.VMEM((SWEEPS, 2, 3, width_x, height), F32),
            pltpu.VMEM((2, 3, width_x, REACH, height), F32),
            pltpu.VMEM((2, 3, width_x, REACH, height), F32),
            pltpu.SemaphoreType.DMA((SWEEPS, 2, 2)),
            pltpu.SemaphoreType.DMA((SWEEPS, 2, 2)),
            pltpu.SemaphoreType.DMA((2, 2)),
            pltpu.SemaphoreType.DMA((2, 2)),
        ],
        compiler_params=pltpu.CompilerParams(
            collective_id=1, has_side_effects=True, vmem_limit_bytes=limit
        ),
    )

    def body(final):
        return pl.pallas_call(
            functools.partial(body_kernel, final),
            name="fit_last" if final else "fit_body",
            out_shape=(shape((3, 3 * slots, points), F32), shape((slots, 128), F32)),
            in_specs=[VM] * 3,
            out_specs=(VM, VM),
            scratch_shapes=[
                pltpu.VMEM((2, 3, slots, points), F32),
                pltpu.VMEM((2, 3, slots, points), F32),
                pltpu.VMEM((3, slots, points), F32),
                pltpu.SemaphoreType.DMA((2, 2)),
                pltpu.SemaphoreType.DMA((2, 2)),
            ],
            compiler_params=pltpu.CompilerParams(
                collective_id=3 if final else 2, has_side_effects=True, vmem_limit_bytes=limit
            ),
        )

    flow = velocity
    motion = None
    for round_index in range(UZ):
        force = scatter(meta, key, depth, lam)
        field = relax(flow, forcing, force, terms)
        flow = field[:, :, REACH:REACH + width_y, :]
        sampled = gather(meta, key, depth, field)
        lam, motion = body(round_index + 1 == UZ)(sampled, radius, lam)
    return flow, motion[:, :6][None, None]


def solution(mesh):
    placed = (
        P(None, "gx", "gy", None),
        P(None, "gx", "gy", None),
        P("gx", "gy", None),
        P("gx", "gy", None, None, None),
        P("gx", "gy", None, None),
        P("gx", "gy", None, None, None),
        P("gx", "gy"),
    )
    return jax.shard_map(
        on_device,
        mesh=mesh,
        in_specs=placed,
        out_specs=(P(None, "gx", "gy", None), P("gx", "gy", None, None)),
        check_vma=False,
    )
```

```python
import functools

import jax
import jax.numpy as jnp
from jax import lax
from jax.experimental import pallas as pl
from jax.experimental.pallas import tpu as pltpu
from jax.sharding import PartitionSpec as P

SWEEPS = 4
UZ = 3
REACH = 8
WINDOW = 24

MASS_TERM = 0.2
VERTICAL_WEIGHT = 0.25
UZAWA_STEP = 0.5

MESH = pl.DeviceIdType.MESH
VM = pl.BlockSpec(memory_space=pltpu.VMEM)
SM = pl.BlockSpec(memory_space=pltpu.SMEM)
F32 = jnp.float32
BF16 = jnp.bfloat16


def around():
    nx, ny = lax.axis_size("gx"), lax.axis_size("gy")
    me_x, me_y = lax.axis_index("gx"), lax.axis_index("gy")
    left = (lax.rem(me_x + nx - 1, nx), me_y)
    right = (lax.rem(me_x + 1, nx), me_y)
    down = (me_x, lax.rem(me_y + ny - 1, ny))
    up = (me_x, lax.rem(me_y + 1, ny))
    return left, right, down, up


def greet(devices):
    barrier = pltpu.get_barrier_semaphore()
    for device in devices:
        pl.semaphore_signal(barrier, inc=1, device_id=device, device_id_type=MESH)
    pl.semaphore_wait(barrier, len(devices))


def send(src, dst, sems, index, device):
    copy = pltpu.make_async_remote_copy(
        src_ref=src,
        dst_ref=dst,
        send_sem=sems.at[0, index],
        recv_sem=sems.at[1, index],
        device_id=device,
        device_id_type=MESH,
    )
    copy.start()
    return copy


def scatter_kernel(meta, key, depth, lam, out):
    width_x = out.shape[1]
    height = out.shape[3]
    rows = width_x * WINDOW
    slots, points = key.shape
    out[...] = jnp.zeros_like(out)

    def one(s, carry):
        @pl.when(meta[1, s] > 0)
        def _():
            base = pl.multiple_of(meta[0, s], 8)
            row_key = key[pl.ds(s, 1), :]
            row_z = depth[pl.ds(s, 1), :]
            mask = lax.broadcasted_iota(jnp.int32, (rows, points), 0) == row_key
            mask = jnp.where(mask, 1.0, 0.0).astype(BF16)
            at_z = lax.broadcasted_iota(jnp.int32, (height, points), 0) == row_z
            high, low = [], []
            for c in range(3):
                value = lam[c, pl.ds(s, 1), :]
                top = value.astype(BF16).astype(F32)
                high.append(jnp.where(at_z, top, 0.0).astype(BF16))
                low.append(jnp.where(at_z, value - top, 0.0).astype(BF16))
            dims = (((1,), (1,)), ((), ()))
            got = lax.dot_general(
                mask, jnp.concatenate(high, 0), dims, preferred_element_type=F32
            ) + lax.dot_general(
                mask, jnp.concatenate(low, 0), dims, preferred_element_type=F32
            )
            for c in range(3):
                part = got[:, c * height:(c + 1) * height].reshape(width_x, WINDOW, height)
                out[c, :, pl.ds(base, WINDOW), :] += part

        return carry

    lax.fori_loop(0, slots, one, 0)


def gather_kernel(meta, key, depth, field, out):
    width_x = field.shape[1]
    height = field.shape[3]
    rows = width_x * WINDOW
    slots, points = key.shape
    out[...] = jnp.zeros_like(out)

    def one(s, carry):
        @pl.when(meta[1, s] > 0)
        def _():
            base = pl.multiple_of(meta[0, s], 8)
            row_key = key[pl.ds(s, 1), :]
            row_z = depth[pl.ds(s, 1), :]
            mask = lax.broadcasted_iota(jnp.int32, (rows, points), 0) == row_key
            at_z = lax.broadcasted_iota(jnp.int32, (height, points), 0) == row_z
            at_z = jnp.where(at_z, 1.0, 0.0).astype(BF16)
            at_z = jnp.concatenate([at_z, at_z], 0)
            for c in range(3):
                value = field[c, :, pl.ds(base, WINDOW), :].reshape(rows, height)
                top = value.astype(BF16)
                rest = (value - top.astype(F32)).astype(BF16)
                got = jnp.dot(
                    jnp.concatenate([top, rest], 1), at_z, preferred_element_type=F32
                )
                out[c, pl.ds(s, 1), :] = jnp.sum(
                    jnp.where(mask, got, 0.0), axis=0, keepdims=True
                )

        return carry

    lax.fori_loop(0, slots, one, 0)


def relax_kernel(
    ghosts, flow, forcing, partial, terms, out, work, source, xh, ys, yh, ph, gh, xsem, ysem, psem, gsem
):
    left, right, down, up = around()
    width_x, width_y, height = forcing.shape[1:]
    lo, hi = REACH, REACH + width_y
    greet((left, right, down, up))
    share = [
        send(partial.at[:, :, pl.ds(0, REACH), :], ph.at[1], psem, 1, down),
        send(partial.at[:, :, pl.ds(hi, REACH), :], ph.at[0], psem, 0, up),
    ]

    def exchange(step, x_ref, first_row, along_y):
        rows = pl.ds(first_row, width_y)
        copies = []
        if along_y:
            for c in range(3):
                ys[step, 1, c] = x_ref[c, :, first_row, :]
                ys[step, 0, c] = x_ref[c, :, first_row + width_y - 1, :]
            copies = [
                send(ys.at[step, 1], yh.at[step, 1], ysem.at[step], 1, down),
                send(ys.at[step, 0], yh.at[step, 0], ysem.at[step], 0, up),
            ]
        return copies + [
            send(x_ref.at[:, 0, rows, :], xh.at[step, 1], xsem.at[step], 1, left),
            send(x_ref.at[:, width_x - 1, rows, :], xh.at[step, 0], xsem.at[step], 0, right),
        ]

    sends = exchange(0, flow, lo if ghosts else 0, not ghosts)
    if ghosts:
        work[0] = flow[...]
    else:
        work[0, :, :, lo:hi, :] = flow[...]
    for copy in share:
        copy.wait()
    source[...] = forcing[...] + partial[:, :, lo:hi, :]
    source[:, :, 0:REACH, :] += ph[0]
    source[:, :, width_y - REACH:width_y, :] += ph[1]
    source[...] = source[...] * terms[6][None]

    for step in range(SWEEPS):
        for copy in sends:
            copy.wait()
        for c in range(3 if step > 0 or not ghosts else 0):
            for i in range(width_x):
                work[step, c, i, lo - 1:lo, :] = yh[step, 0, c, i:i + 1, :]
                work[step, c, i, hi:hi + 1, :] = yh[step, 1, c, i:i + 1, :]
        target = work.at[step + 1] if step + 1 < SWEEPS else out

        def component(c, carry):
            for i in range(width_x):
                here = work[step, c, i, lo:hi, :]
                west = xh[step, 0, c] if i == 0 else work[step, c, i - 1, lo:hi, :]
                east = xh[step, 1, c] if i == width_x - 1 else work[step, c, i + 1, lo:hi, :]
                south = work[step, c, i, lo - 1:hi - 1, :]
                north = work[step, c, i, lo + 1:hi + 1, :]
                target[c, i, lo:hi, :] = (
                    source[c, i]
                    + terms[0, i] * west
                    + terms[1, i] * east
                    + terms[2, i] * south
                    + terms[3, i] * north
                    + terms[4, i] * pltpu.roll(here, 1, 1)
                    + terms[5, i] * pltpu.roll(here, height - 1, 1)
                )
            return carry

        lax.fori_loop(0, 3, component, 0)
        if step + 1 < SWEEPS:
            sends = exchange(step + 1, target, lo, True)

    last = [
        send(out.at[:, :, pl.ds(lo, REACH), :], gh.at[1], gsem, 1, down),
        send(out.at[:, :, pl.ds(hi - REACH, REACH), :], gh.at[0], gsem, 0, up),
    ]
    for copy in last:
        copy.wait()
    out[:, :, 0:lo, :] = gh[0]
    out[:, :, hi:hi + REACH, :] = gh[1]


def fit(w, r, points):
    spread = jnp.sum(r[0] * r[0] + r[1] * r[1] + r[2] * r[2], axis=1, keepdims=True)
    mean = [jnp.sum(w[c], axis=1, keepdims=True) / points for c in range(3)]
    spin = []
    for c in range(3):
        a, b = (c + 1) % 3, (c + 2) % 3
        moment = jnp.sum(r[a] * w[b] - r[b] * w[a], axis=1, keepdims=True)
        spin.append(1.5 * moment / spread)
    return mean, spin


def update_kernel(sampled, radius, lam, out, near_left, near_right, far_left, far_right, sems):
    left, right, _, _ = around()
    count = lax.axis_size("gx")
    far_down = (lax.rem(left[0] + count - 1, count), left[1])
    far_up = (lax.rem(right[0] + 1, count), right[1])
    slots, points = radius.shape[1] // 3, radius.shape[2]
    greet((left, right, far_down, far_up))
    sends = [
        send(sampled.at[:, pl.ds(0, slots), :], far_right, sems, 3, far_down),
        send(sampled.at[:, pl.ds(2 * slots, slots), :], far_left, sems, 2, far_up),
        send(sampled.at[:, pl.ds(0, 2 * slots), :], near_right, sems, 1, left),
        send(sampled.at[:, pl.ds(slots, 2 * slots), :], near_left, sems, 0, right),
    ]
    r = [radius[c] for c in range(3)]
    for copy in sends:
        copy.wait()
    w = []
    for c in range(3):
        first = near_left[c, 0:slots, :] + far_left[c]
        middle = near_left[c, slots:2 * slots, :] + near_right[c, 0:slots, :]
        last = near_right[c, slots:2 * slots, :] + far_right[c]
        w.append(sampled[c] + jnp.concatenate([first, middle, last], 0))
    mean, spin = fit(w, r, points)
    for c in range(3):
        a, b = (c + 1) % 3, (c + 2) % 3
        target = mean[c] + (spin[a] * r[b] - spin[b] * r[a])
        out[c] = lam[c] + UZAWA_STEP * (target - w[c])


def motion_kernel(sampled, radius, motion, wh, sems):
    left, right, _, _ = around()
    slots, points = radius.shape[1] // 3, radius.shape[2]
    greet((left, right))
    sends = [
        send(sampled.at[:, pl.ds(0, slots), :], wh.at[1], sems, 1, left),
        send(sampled.at[:, pl.ds(2 * slots, slots), :], wh.at[0], sems, 0, right),
    ]
    r = [radius[c, slots:2 * slots, :] for c in range(3)]
    for copy in sends:
        copy.wait()
    w = [sampled[c, slots:2 * slots, :] + wh[0, c] + wh[1, c] for c in range(3)]
    mean, spin = fit(w, r, points)
    lane = lax.broadcasted_iota(jnp.int32, motion.shape, 1)
    row = jnp.zeros(motion.shape, F32)
    for c, value in enumerate(mean + spin):
        row = jnp.where(lane == c, value, row)
    motion[...] = row


def pair(block, axis, dim, width):
    count = lax.axis_size(axis)
    forward = [(i, (i + 1) % count) for i in range(count)]
    backward = [(target, source) for source, target in forward]
    size = block.shape[dim]
    low = lax.ppermute(lax.slice_in_dim(block, size - width, size, axis=dim), axis, forward)
    high = lax.ppermute(lax.slice_in_dim(block, 0, width, axis=dim), axis, backward)
    return jnp.concatenate([low, block, high], axis=dim)


def face_terms(nu):
    along_x = pair(nu, "gx", 0, 1)
    along_y = pair(nu, "gy", 1, 1)
    along_z = jnp.concatenate([nu[:, :, :1], nu, nu[:, :, -1:]], axis=2)
    k = [
        0.5 * (nu + along_x[:-2]),
        0.5 * (nu + along_x[2:]),
        0.5 * (nu + along_y[:, :-2]),
        0.5 * (nu + along_y[:, 2:]),
        VERTICAL_WEIGHT * 0.5 * (nu + along_z[:, :, :-2]),
        VERTICAL_WEIGHT * 0.5 * (nu + along_z[:, :, 2:]),
    ]
    inverse = 1.0 / (MASS_TERM + k[0] + k[1] + k[2] + k[3] + k[4] + k[5])
    z = jnp.arange(nu.shape[2])
    k[4] = jnp.where(z == 0, 0.0, k[4])
    k[5] = jnp.where(z == nu.shape[2] - 1, 0.0, k[5])
    return jnp.stack([face * inverse for face in k] + [inverse])


def on_device(
    velocity, forcing, viscosity, multipliers, sphere_centres, sphere_offsets, sphere_count
):
    _, width_x, width_y, height = velocity.shape
    slots, points = multipliers.shape[2], multipliers.shape[4]
    live = jnp.arange(slots) < sphere_count[0, 0]
    centres = sphere_centres[0, 0]
    offsets = jnp.moveaxis(sphere_offsets[0, 0], 1, 0)
    base = (centres[:, 1] // 8) * 8
    own_x = jnp.where(live[:, None], centres[:, 0:1] + offsets[0], -8 * width_x)
    own_y = (centres[:, 1] - base)[:, None] + offsets[1] + REACH
    own_z = centres[:, 2:3] + offsets[2]
    geometry = jnp.stack(
        [own_x, own_y, own_z, jnp.broadcast_to(base[:, None], own_x.shape), *offsets]
    ).astype(jnp.int32)
    near = pair(geometry, "gx", 1, slots)
    shift = jnp.repeat((jnp.arange(3) - 1) * width_x, slots)[:, None]
    local_x = near[0] + shift
    inside = (local_x >= 0) & (local_x < width_x)
    key = jnp.where(inside, local_x * WINDOW + near[1], -1).astype(jnp.int32)
    depth = near[2]
    meta = jnp.stack([near[3, :, 0], jnp.any(inside, 1).astype(jnp.int32)])
    radius = near[4:7].astype(F32)
    lam = pair(jnp.moveaxis(multipliers[0, 0], 1, 0), "gx", 1, slots)
    terms = face_terms(viscosity)

    wide = (3, width_x, width_y + 2 * REACH, height)
    shape = jax.ShapeDtypeStruct
    limit = 48 * 1024 * 1024
    scatter = pl.pallas_call(
        scatter_kernel,
        name="spread_force",
        out_shape=shape(wide, F32),
        in_specs=[SM, VM, VM, VM],
        out_specs=VM,
        compiler_params=pltpu.CompilerParams(vmem_limit_bytes=limit),
    )
    gather = pl.pallas_call(
        gather_kernel,
        name="sample_flow",
        out_shape=shape((3, 3 * slots, points), F32),
        in_specs=[SM, VM, VM, VM],
        out_specs=VM,
        compiler_params=pltpu.CompilerParams(vmem_limit_bytes=limit),
    )
    def relax(ghosts):
        return pl.pallas_call(
            functools.partial(relax_kernel, ghosts),
            name="relax_ghosts" if ghosts else "relax_first",
            out_shape=shape(wide, F32),
            in_specs=[VM] * 4,
            out_specs=VM,
            scratch_shapes=[
                pltpu.VMEM((SWEEPS,) + wide, F32),
                pltpu.VMEM((3, width_x, width_y, height), F32),
                pltpu.VMEM((SWEEPS, 2, 3, width_y, height), F32),
                pltpu.VMEM((SWEEPS, 2, 3, width_x, height), F32),
                pltpu.VMEM((SWEEPS, 2, 3, width_x, height), F32),
                pltpu.VMEM((2, 3, width_x, REACH, height), F32),
                pltpu.VMEM((2, 3, width_x, REACH, height), F32),
                pltpu.SemaphoreType.DMA((SWEEPS, 2, 2)),
                pltpu.SemaphoreType.DMA((SWEEPS, 2, 2)),
                pltpu.SemaphoreType.DMA((2, 2)),
                pltpu.SemaphoreType.DMA((2, 2)),
            ],
            compiler_params=pltpu.CompilerParams(
                collective_id=4 if ghosts else 1, has_side_effects=True, vmem_limit_bytes=limit
            ),
        )

    update = pl.pallas_call(
        update_kernel,
        name="fit_update",
        out_shape=shape((3, 3 * slots, points), F32),
        in_specs=[VM] * 3,
        out_specs=VM,
        scratch_shapes=[
            pltpu.VMEM((3, 2 * slots, points), F32),
            pltpu.VMEM((3, 2 * slots, points), F32),
            pltpu.VMEM((3, slots, points), F32),
            pltpu.VMEM((3, slots, points), F32),
            pltpu.SemaphoreType.DMA((2, 4)),
        ],
        compiler_params=pltpu.CompilerParams(
            collective_id=2, has_side_effects=True, vmem_limit_bytes=limit
        ),
    )
    conclude = pl.pallas_call(
        motion_kernel,
        name="fit_motion",
        out_shape=shape((slots, 128), F32),
        in_specs=[VM] * 2,
        out_specs=VM,
        scratch_shapes=[
            pltpu.VMEM((2, 3, slots, points), F32),
            pltpu.SemaphoreType.DMA((2, 2)),
        ],
        compiler_params=pltpu.CompilerParams(
            collective_id=3, has_side_effects=True, vmem_limit_bytes=limit
        ),
    )

    field = velocity
    for round_index in range(UZ):
        force = scatter(meta, key, depth, lam)
        field = relax(round_index > 0)(field, forcing, force, terms)
        sampled = gather(meta, key, depth, field)
        if round_index + 1 < UZ:
            lam = update(sampled, radius, lam)
    motion = conclude(sampled, radius)
    return field[:, :, REACH:REACH + width_y, :], motion[:, :6][None, None]


def solution(mesh):
    placed = (
        P(None, "gx", "gy", None),
        P(None, "gx", "gy", None),
        P("gx", "gy", None),
        P("gx", "gy", None, None, None),
        P("gx", "gy", None, None),
        P("gx", "gy", None, None, None),
        P("gx", "gy"),
    )
    return jax.shard_map(
        on_device,
        mesh=mesh,
        in_specs=placed,
        out_specs=(P(None, "gx", "gy", None), P("gx", "gy", None, None)),
        check_vma=False,
    )
```

```python
import functools

import jax
import jax.numpy as jnp
from jax import lax
from jax.experimental import pallas as pl
from jax.experimental.pallas import tpu as pltpu
from jax.sharding import PartitionSpec as P

SWEEPS = 4
UZ = 3
REACH = 8
WINDOW = 24

MASS_TERM = 0.2
VERTICAL_WEIGHT = 0.25
UZAWA_STEP = 0.5

MESH = pl.DeviceIdType.MESH
VM = pl.BlockSpec(memory_space=pltpu.VMEM)
SM = pl.BlockSpec(memory_space=pltpu.SMEM)
F32 = jnp.float32
BF16 = jnp.bfloat16


def around():
    nx, ny = lax.axis_size("gx"), lax.axis_size("gy")
    me_x, me_y = lax.axis_index("gx"), lax.axis_index("gy")
    left = (lax.rem(me_x + nx - 1, nx), me_y)
    right = (lax.rem(me_x + 1, nx), me_y)
    down = (me_x, lax.rem(me_y + ny - 1, ny))
    up = (me_x, lax.rem(me_y + 1, ny))
    return left, right, down, up


def greet(devices):
    barrier = pltpu.get_barrier_semaphore()
    for device in devices:
        pl.semaphore_signal(barrier, inc=1, device_id=device, device_id_type=MESH)
    pl.semaphore_wait(barrier, len(devices))


def send(src, dst, sems, index, device):
    copy = pltpu.make_async_remote_copy(
        src_ref=src,
        dst_ref=dst,
        send_sem=sems.at[0, index],
        recv_sem=sems.at[1, index],
        device_id=device,
        device_id_type=MESH,
    )
    copy.start()
    return copy


def scatter_kernel(meta, key, depth, lam, out):
    width_x = out.shape[1]
    height = out.shape[3]
    rows = width_x * WINDOW
    slots, points = key.shape
    out[...] = jnp.zeros_like(out)

    def one(s, carry):
        @pl.when(meta[s, 1] > 0)
        def _():
            base = pl.multiple_of(meta[s, 0], 8)
            row_key = key[pl.ds(s, 1), :]
            row_z = depth[pl.ds(s, 1), :]
            mask = lax.broadcasted_iota(jnp.int32, (rows, points), 0) == row_key
            mask = jnp.where(mask, 1.0, 0.0).astype(BF16)
            at_z = lax.broadcasted_iota(jnp.int32, (height, points), 0) == row_z
            high, low = [], []
            for c in range(3):
                value = lam[c, pl.ds(s, 1), :]
                top = value.astype(BF16).astype(F32)
                high.append(jnp.where(at_z, top, 0.0).astype(BF16))
                low.append(jnp.where(at_z, value - top, 0.0).astype(BF16))
            dims = (((1,), (1,)), ((), ()))
            got = lax.dot_general(
                mask, jnp.concatenate(high, 0), dims, preferred_element_type=F32
            ) + lax.dot_general(
                mask, jnp.concatenate(low, 0), dims, preferred_element_type=F32
            )
            for c in range(3):
                part = got[:, c * height:(c + 1) * height].reshape(width_x, WINDOW, height)
                out[c, :, pl.ds(base, WINDOW), :] += part

        return carry

    lax.fori_loop(0, slots, one, 0)


def gather_kernel(meta, key, depth, field, out):
    width_x = field.shape[1]
    height = field.shape[3]
    rows = width_x * WINDOW
    slots, points = key.shape
    out[...] = jnp.zeros_like(out)

    def one(s, carry):
        @pl.when(meta[s, 1] > 0)
        def _():
            base = pl.multiple_of(meta[s, 0], 8)
            row_key = key[pl.ds(s, 1), :]
            row_z = depth[pl.ds(s, 1), :]
            mask = lax.broadcasted_iota(jnp.int32, (rows, points), 0) == row_key
            at_z = lax.broadcasted_iota(jnp.int32, (height, points), 0) == row_z
            at_z = jnp.where(at_z, 1.0, 0.0).astype(BF16)
            at_z = jnp.concatenate([at_z, at_z], 0)
            for c in range(3):
                value = field[c, :, pl.ds(base, WINDOW), :].reshape(rows, height)
                top = value.astype(BF16)
                rest = (value - top.astype(F32)).astype(BF16)
                got = jnp.dot(
                    jnp.concatenate([top, rest], 1), at_z, preferred_element_type=F32
                )
                out[c, pl.ds(s, 1), :] = jnp.sum(
                    jnp.where(mask, got, 0.0), axis=0, keepdims=True
                )

        return carry

    lax.fori_loop(0, slots, one, 0)


def relax_kernel(
    ghosts, flow, forcing, partial, terms, out, work, source, xh, ys, yh, ph, gh, xsem, ysem, psem, gsem
):
    left, right, down, up = around()
    width_x, width_y, height = forcing.shape[1:]
    lo, hi = REACH, REACH + width_y
    greet((left, right, down, up))
    share = [
        send(partial.at[:, :, pl.ds(0, REACH), :], ph.at[1], psem, 1, down),
        send(partial.at[:, :, pl.ds(hi, REACH), :], ph.at[0], psem, 0, up),
    ]

    def exchange(step, x_ref, first_row, along_y):
        rows = pl.ds(first_row, width_y)
        copies = []
        if along_y:
            for c in range(3):
                ys[step, 1, c] = x_ref[c, :, first_row, :]
                ys[step, 0, c] = x_ref[c, :, first_row + width_y - 1, :]
            copies = [
                send(ys.at[step, 1], yh.at[step, 1], ysem.at[step], 1, down),
                send(ys.at[step, 0], yh.at[step, 0], ysem.at[step], 0, up),
            ]
        return copies + [
            send(x_ref.at[:, 0, rows, :], xh.at[step, 1], xsem.at[step], 1, left),
            send(x_ref.at[:, width_x - 1, rows, :], xh.at[step, 0], xsem.at[step], 0, right),
        ]

    sends = exchange(0, flow, lo if ghosts else 0, not ghosts)
    if ghosts:
        work[0] = flow[...]
    else:
        work[0, :, :, lo:hi, :] = flow[...]
    for copy in share:
        copy.wait()
    source[...] = forcing[...] + partial[:, :, lo:hi, :]
    source[:, :, 0:REACH, :] += ph[0]
    source[:, :, width_y - REACH:width_y, :] += ph[1]
    source[...] = source[...] * terms[6][None]

    for step in range(SWEEPS):
        for copy in sends:
            copy.wait()
        for c in range(3 if step > 0 or not ghosts else 0):
            for i in range(width_x):
                work[step, c, i, lo - 1:lo, :] = yh[step, 0, c, i:i + 1, :]
                work[step, c, i, hi:hi + 1, :] = yh[step, 1, c, i:i + 1, :]
        target = work.at[step + 1] if step + 1 < SWEEPS else out

        def component(c, carry):
            for i in range(width_x):
                here = work[step, c, i, lo:hi, :]
                west = xh[step, 0, c] if i == 0 else work[step, c, i - 1, lo:hi, :]
                east = xh[step, 1, c] if i == width_x - 1 else work[step, c, i + 1, lo:hi, :]
                south = work[step, c, i, lo - 1:hi - 1, :]
                north = work[step, c, i, lo + 1:hi + 1, :]
                target[c, i, lo:hi, :] = (
                    source[c, i]
                    + terms[0, i] * west
                    + terms[1, i] * east
                    + terms[2, i] * south
                    + terms[3, i] * north
                    + terms[4, i] * pltpu.roll(here, 1, 1)
                    + terms[5, i] * pltpu.roll(here, height - 1, 1)
                )
            return carry

        lax.fori_loop(0, 3, component, 0)
        if step + 1 < SWEEPS:
            sends = exchange(step + 1, target, lo, True)

    last = [
        send(out.at[:, :, pl.ds(lo, REACH), :], gh.at[1], gsem, 1, down),
        send(out.at[:, :, pl.ds(hi - REACH, REACH), :], gh.at[0], gsem, 0, up),
    ]
    for copy in last:
        copy.wait()
    out[:, :, 0:lo, :] = gh[0]
    out[:, :, hi:hi + REACH, :] = gh[1]


def fit(w, r, points):
    spread = jnp.sum(r[0] * r[0] + r[1] * r[1] + r[2] * r[2], axis=1, keepdims=True)
    mean = [jnp.sum(w[c], axis=1, keepdims=True) / points for c in range(3)]
    spin = []
    for c in range(3):
        a, b = (c + 1) % 3, (c + 2) % 3
        moment = jnp.sum(r[a] * w[b] - r[b] * w[a], axis=1, keepdims=True)
        spin.append(1.5 * moment / spread)
    return mean, spin


def update_kernel(sampled, radius, lam, out, near_left, near_right, far_left, far_right, sems):
    left, right, _, _ = around()
    count = lax.axis_size("gx")
    far_down = (lax.rem(left[0] + count - 1, count), left[1])
    far_up = (lax.rem(right[0] + 1, count), right[1])
    slots, points = radius.shape[1] // 3, radius.shape[2]
    greet((left, right, far_down, far_up))
    sends = [
        send(sampled.at[:, pl.ds(0, slots), :], far_right, sems, 3, far_down),
        send(sampled.at[:, pl.ds(2 * slots, slots), :], far_left, sems, 2, far_up),
        send(sampled.at[:, pl.ds(0, 2 * slots), :], near_right, sems, 1, left),
        send(sampled.at[:, pl.ds(slots, 2 * slots), :], near_left, sems, 0, right),
    ]
    r = [radius[c] for c in range(3)]
    for copy in sends:
        copy.wait()
    w = []
    for c in range(3):
        first = near_left[c, 0:slots, :] + far_left[c]
        middle = near_left[c, slots:2 * slots, :] + near_right[c, 0:slots, :]
        last = near_right[c, slots:2 * slots, :] + far_right[c]
        w.append(sampled[c] + jnp.concatenate([first, middle, last], 0))
    mean, spin = fit(w, r, points)
    for c in range(3):
        a, b = (c + 1) % 3, (c + 2) % 3
        target = mean[c] + (spin[a] * r[b] - spin[b] * r[a])
        out[c] = lam[c] + UZAWA_STEP * (target - w[c])


def motion_kernel(sampled, radius, motion, wh, sems):
    left, right, _, _ = around()
    slots, points = radius.shape[1] // 3, radius.shape[2]
    greet((left, right))
    sends = [
        send(sampled.at[:, pl.ds(0, slots), :], wh.at[1], sems, 1, left),
        send(sampled.at[:, pl.ds(2 * slots, slots), :], wh.at[0], sems, 0, right),
    ]
    r = [radius[c, slots:2 * slots, :] for c in range(3)]
    for copy in sends:
        copy.wait()
    w = [sampled[c, slots:2 * slots, :] + wh[0, c] + wh[1, c] for c in range(3)]
    mean, spin = fit(w, r, points)
    lane = lax.broadcasted_iota(jnp.int32, motion.shape, 1)
    row = jnp.zeros(motion.shape, F32)
    for c, value in enumerate(mean + spin):
        row = jnp.where(lane == c, value, row)
    motion[...] = row


def setup_kernel(
    nu, geometry, lam, terms, key, depth, radius, meta, lam_out, xh, ys, yh, gh, lh, sems
):
    left, right, down, up = around()
    width_x, width_y, height = nu.shape
    slots = geometry.shape[1]
    greet((left, right, down, up))
    ys[1] = nu[:, 0, :]
    ys[0] = nu[:, width_y - 1, :]
    sends = [
        send(ys.at[1], yh.at[1], sems, 0, down),
        send(ys.at[0], yh.at[0], sems, 1, up),
        send(nu.at[0], xh.at[1], sems, 2, left),
        send(nu.at[width_x - 1], xh.at[0], sems, 3, right),
        send(geometry, gh.at[1], sems, 4, left),
        send(geometry, gh.at[0], sems, 5, right),
        send(lam, lh.at[1], sems, 6, left),
        send(lam, lh.at[0], sems, 7, right),
    ]
    for copy in sends:
        copy.wait()
    z = lax.broadcasted_iota(jnp.int32, (width_y, height), 1)
    for i in range(width_x):
        here = nu[i]
        west = xh[0] if i == 0 else nu[i - 1]
        east = xh[1] if i == width_x - 1 else nu[i + 1]
        south = jnp.concatenate([yh[0, i:i + 1, :], here[:-1]], 0)
        north = jnp.concatenate([here[1:], yh[1, i:i + 1, :]], 0)
        below = jnp.where(z == 0, here, pltpu.roll(here, 1, 1))
        above = jnp.where(z == height - 1, here, pltpu.roll(here, height - 1, 1))
        k = [0.5 * (here + side) for side in (west, east, south, north)]
        k += [VERTICAL_WEIGHT * 0.5 * (here + side) for side in (below, above)]
        inverse = 1.0 / (MASS_TERM + k[0] + k[1] + k[2] + k[3] + k[4] + k[5])
        k[4] = jnp.where(z == 0, 0.0, k[4])
        k[5] = jnp.where(z == height - 1, 0.0, k[5])
        for f in range(6):
            terms[f, i] = k[f] * inverse
        terms[6, i] = inverse
    lane = lax.broadcasted_iota(jnp.int32, (slots, meta.shape[1]), 1)
    groups = (gh.at[0], geometry, gh.at[1])
    values = (lh.at[0], lam, lh.at[1])
    for g in range(3):
        part = groups[g]
        rows = slice(g * slots, (g + 1) * slots)
        local_x = part[0] + (g - 1) * width_x
        inside = (local_x >= 0) & (local_x < width_x)
        key[rows, :] = jnp.where(inside, local_x * WINDOW + part[1], -1)
        depth[rows, :] = part[2]
        active = jnp.max(jnp.where(inside, 1.0, 0.0), axis=1, keepdims=True).astype(jnp.int32)
        meta[rows, :] = jnp.where(lane == 0, part[3, :, 0:1], active)
        for c in range(3):
            radius[c, rows, :] = part[4 + c].astype(F32)
            lam_out[c, rows, :] = values[g][c]


def on_device(
    velocity, forcing, viscosity, multipliers, sphere_centres, sphere_offsets, sphere_count
):
    _, width_x, width_y, height = velocity.shape
    slots, points = multipliers.shape[2], multipliers.shape[4]
    live = jnp.arange(slots) < sphere_count[0, 0]
    centres = sphere_centres[0, 0]
    offsets = jnp.moveaxis(sphere_offsets[0, 0], 1, 0)
    base = (centres[:, 1] // 8) * 8
    own_x = jnp.where(live[:, None], centres[:, 0:1] + offsets[0], -8 * width_x)
    own_y = (centres[:, 1] - base)[:, None] + offsets[1] + REACH
    own_z = centres[:, 2:3] + offsets[2]
    geometry = jnp.stack(
        [own_x, own_y, own_z, jnp.broadcast_to(base[:, None], own_x.shape), *offsets]
    ).astype(jnp.int32)
    wide = (3, width_x, width_y + 2 * REACH, height)
    shape = jax.ShapeDtypeStruct
    limit = 48 * 1024 * 1024
    scatter = pl.pallas_call(
        scatter_kernel,
        name="spread_force",
        out_shape=shape(wide, F32),
        in_specs=[SM, VM, VM, VM],
        out_specs=VM,
        compiler_params=pltpu.CompilerParams(vmem_limit_bytes=limit),
    )
    gather = pl.pallas_call(
        gather_kernel,
        name="sample_flow",
        out_shape=shape((3, 3 * slots, points), F32),
        in_specs=[SM, VM, VM, VM],
        out_specs=VM,
        compiler_params=pltpu.CompilerParams(vmem_limit_bytes=limit),
    )
    def relax(ghosts):
        return pl.pallas_call(
            functools.partial(relax_kernel, ghosts),
            name="relax_ghosts" if ghosts else "relax_first",
            out_shape=shape(wide, F32),
            in_specs=[VM] * 4,
            out_specs=VM,
            scratch_shapes=[
                pltpu.VMEM((SWEEPS,) + wide, F32),
                pltpu.VMEM((3, width_x, width_y, height), F32),
                pltpu.VMEM((SWEEPS, 2, 3, width_y, height), F32),
                pltpu.VMEM((SWEEPS, 2, 3, width_x, height), F32),
                pltpu.VMEM((SWEEPS, 2, 3, width_x, height), F32),
                pltpu.VMEM((2, 3, width_x, REACH, height), F32),
                pltpu.VMEM((2, 3, width_x, REACH, height), F32),
                pltpu.SemaphoreType.DMA((SWEEPS, 2, 2)),
                pltpu.SemaphoreType.DMA((SWEEPS, 2, 2)),
                pltpu.SemaphoreType.DMA((2, 2)),
                pltpu.SemaphoreType.DMA((2, 2)),
            ],
            compiler_params=pltpu.CompilerParams(
                collective_id=4 if ghosts else 1, has_side_effects=True, vmem_limit_bytes=limit
            ),
        )

    update = pl.pallas_call(
        update_kernel,
        name="fit_update",
        out_shape=shape((3, 3 * slots, points), F32),
        in_specs=[VM] * 3,
        out_specs=VM,
        scratch_shapes=[
            pltpu.VMEM((3, 2 * slots, points), F32),
            pltpu.VMEM((3, 2 * slots, points), F32),
            pltpu.VMEM((3, slots, points), F32),
            pltpu.VMEM((3, slots, points), F32),
            pltpu.SemaphoreType.DMA((2, 4)),
        ],
        compiler_params=pltpu.CompilerParams(
            collective_id=2, has_side_effects=True, vmem_limit_bytes=limit
        ),
    )
    conclude = pl.pallas_call(
        motion_kernel,
        name="fit_motion",
        out_shape=shape((slots, 128), F32),
        in_specs=[VM] * 2,
        out_specs=VM,
        scratch_shapes=[
            pltpu.VMEM((2, 3, slots, points), F32),
            pltpu.SemaphoreType.DMA((2, 2)),
        ],
        compiler_params=pltpu.CompilerParams(
            collective_id=3, has_side_effects=True, vmem_limit_bytes=limit
        ),
    )

    prepare = pl.pallas_call(
        setup_kernel,
        name="prepare",
        out_shape=(
            shape((7, width_x, width_y, height), F32),
            shape((3 * slots, points), jnp.int32),
            shape((3 * slots, points), jnp.int32),
            shape((3, 3 * slots, points), F32),
            shape((3 * slots, 128), jnp.int32),
            shape((3, 3 * slots, points), F32),
        ),
        in_specs=[VM] * 3,
        out_specs=(VM,) * 6,
        scratch_shapes=[
            pltpu.VMEM((2, width_y, height), F32),
            pltpu.VMEM((2, width_x, height), F32),
            pltpu.VMEM((2, width_x, height), F32),
            pltpu.VMEM((2, 7, slots, points), jnp.int32),
            pltpu.VMEM((2, 3, slots, points), F32),
            pltpu.SemaphoreType.DMA((2, 8)),
        ],
        compiler_params=pltpu.CompilerParams(
            collective_id=5, has_side_effects=True, vmem_limit_bytes=limit
        ),
    )
    terms, key, depth, radius, meta, lam = prepare(
        viscosity, geometry, jnp.moveaxis(multipliers[0, 0], 1, 0)
    )
    field = velocity
    for round_index in range(UZ):
        force = scatter(meta, key, depth, lam)
        field = relax(round_index > 0)(field, forcing, force, terms)
        sampled = gather(meta, key, depth, field)
        if round_index + 1 < UZ:
            lam = update(sampled, radius, lam)
    motion = conclude(sampled, radius)
    return field[:, :, REACH:REACH + width_y, :], motion[:, :6][None, None]


def solution(mesh):
    placed = (
        P(None, "gx", "gy", None),
        P(None, "gx", "gy", None),
        P("gx", "gy", None),
        P("gx", "gy", None, None, None),
        P("gx", "gy", None, None),
        P("gx", "gy", None, None, None),
        P("gx", "gy"),
    )
    return jax.shard_map(
        on_device,
        mesh=mesh,
        in_specs=placed,
        out_specs=(P(None, "gx", "gy", None), P("gx", "gy", None, None)),
        check_vma=False,
    )
```

```python
import functools

import jax
import jax.numpy as jnp
from jax import lax
from jax.experimental import pallas as pl
from jax.experimental.pallas import tpu as pltpu
from jax.sharding import PartitionSpec as P

SWEEPS = 4
UZ = 3
REACH = 8
WINDOW = 24

MASS_TERM = 0.2
VERTICAL_WEIGHT = 0.25
UZAWA_STEP = 0.5

MESH = pl.DeviceIdType.MESH
VM = pl.BlockSpec(memory_space=pltpu.VMEM)
SM = pl.BlockSpec(memory_space=pltpu.SMEM)
F32 = jnp.float32
BF16 = jnp.bfloat16


def around():
    nx, ny = lax.axis_size("gx"), lax.axis_size("gy")
    me_x, me_y = lax.axis_index("gx"), lax.axis_index("gy")
    left = (lax.rem(me_x + nx - 1, nx), me_y)
    right = (lax.rem(me_x + 1, nx), me_y)
    down = (me_x, lax.rem(me_y + ny - 1, ny))
    up = (me_x, lax.rem(me_y + 1, ny))
    return left, right, down, up


def greet(devices):
    barrier = pltpu.get_barrier_semaphore()
    for device in devices:
        pl.semaphore_signal(barrier, inc=1, device_id=device, device_id_type=MESH)
    pl.semaphore_wait(barrier, len(devices))


def send(src, dst, sems, index, device):
    copy = pltpu.make_async_remote_copy(
        src_ref=src,
        dst_ref=dst,
        send_sem=sems.at[0, index],
        recv_sem=sems.at[1, index],
        device_id=device,
        device_id_type=MESH,
    )
    copy.start()
    return copy


def scatter_kernel(meta, key, depth, lam, out):
    width_x = out.shape[1]
    height = out.shape[3]
    rows = width_x * WINDOW
    slots, points = key.shape
    out[...] = jnp.zeros_like(out)

    def one(s, carry):
        @pl.when(meta[s, 1] > 0)
        def _():
            base = pl.multiple_of(meta[s, 0], 8)
            row_key = key[pl.ds(s, 1), :]
            row_z = depth[pl.ds(s, 1), :]
            mask = lax.broadcasted_iota(jnp.int32, (rows, points), 0) == row_key
            mask = jnp.where(mask, 1.0, 0.0).astype(BF16)
            at_z = lax.broadcasted_iota(jnp.int32, (height, points), 0) == row_z
            at_z = jnp.where(at_z, 1.0, 0.0).astype(BF16)
            high, low = [], []
            for c in range(3):
                value = lam[c, pl.ds(s, 1), :]
                top = value.astype(BF16)
                rest = (value - top.astype(F32)).astype(BF16)
                high.append(at_z * top)
                low.append(at_z * rest)
            dims = (((1,), (1,)), ((), ()))
            got = lax.dot_general(
                mask, jnp.concatenate(high, 0), dims, preferred_element_type=F32
            ) + lax.dot_general(
                mask, jnp.concatenate(low, 0), dims, preferred_element_type=F32
            )
            for c in range(3):
                part = got[:, c * height:(c + 1) * height].reshape(width_x, WINDOW, height)
                out[c, :, pl.ds(base, WINDOW), :] += part

        return carry

    lax.fori_loop(0, slots, one, 0)


def gather_kernel(meta, key, depth, field, out):
    width_x = field.shape[1]
    height = field.shape[3]
    rows = width_x * WINDOW
    slots, points = key.shape
    out[...] = jnp.zeros_like(out)

    def one(s, carry):
        @pl.when(meta[s, 1] > 0)
        def _():
            base = pl.multiple_of(meta[s, 0], 8)
            row_key = key[pl.ds(s, 1), :]
            row_z = depth[pl.ds(s, 1), :]
            mask = lax.broadcasted_iota(jnp.int32, (rows, points), 0) == row_key
            at_z = lax.broadcasted_iota(jnp.int32, (height, points), 0) == row_z
            at_z = jnp.where(at_z, 1.0, 0.0).astype(BF16)
            at_z = jnp.concatenate([at_z, at_z], 0)
            for c in range(3):
                value = field[c, :, pl.ds(base, WINDOW), :].reshape(rows, height)
                top = value.astype(BF16)
                rest = (value - top.astype(F32)).astype(BF16)
                got = jnp.dot(
                    jnp.concatenate([top, rest], 1), at_z, preferred_element_type=F32
                )
                out[c, pl.ds(s, 1), :] = jnp.sum(
                    jnp.where(mask, got, 0.0), axis=0, keepdims=True
                )

        return carry

    lax.fori_loop(0, slots, one, 0)


def relax_kernel(
    ghosts, flow, forcing, partial, terms, out, work, source, xh, ys, yh, ph, gh, xsem, ysem, psem, gsem
):
    left, right, down, up = around()
    width_x, width_y, height = forcing.shape[1:]
    lo, hi = REACH, REACH + width_y
    greet((left, right, down, up))
    share = [
        send(partial.at[:, :, pl.ds(0, REACH), :], ph.at[1], psem, 1, down),
        send(partial.at[:, :, pl.ds(hi, REACH), :], ph.at[0], psem, 0, up),
    ]

    def exchange(step, x_ref, first_row, along_y):
        rows = pl.ds(first_row, width_y)
        copies = []
        if along_y:
            for c in range(3):
                ys[step, 1, c] = x_ref[c, :, first_row, :]
                ys[step, 0, c] = x_ref[c, :, first_row + width_y - 1, :]
            copies = [
                send(ys.at[step, 1], yh.at[step, 1], ysem.at[step], 1, down),
                send(ys.at[step, 0], yh.at[step, 0], ysem.at[step], 0, up),
            ]
        return copies + [
            send(x_ref.at[:, 0, rows, :], xh.at[step, 1], xsem.at[step], 1, left),
            send(x_ref.at[:, width_x - 1, rows, :], xh.at[step, 0], xsem.at[step], 0, right),
        ]

    sends = exchange(0, flow, lo if ghosts else 0, not ghosts)
    if ghosts:
        work[0] = flow[...]
    else:
        work[0, :, :, lo:hi, :] = flow[...]
    for copy in share:
        copy.wait()
    source[...] = forcing[...] + partial[:, :, lo:hi, :]
    source[:, :, 0:REACH, :] += ph[0]
    source[:, :, width_y - REACH:width_y, :] += ph[1]
    source[...] = source[...] * terms[6][None]

    for step in range(SWEEPS):
        for copy in sends:
            copy.wait()
        for c in range(3 if step > 0 or not ghosts else 0):
            for i in range(width_x):
                work[step, c, i, lo - 1:lo, :] = yh[step, 0, c, i:i + 1, :]
                work[step, c, i, hi:hi + 1, :] = yh[step, 1, c, i:i + 1, :]
        target = work.at[step + 1] if step + 1 < SWEEPS else out

        def component(c, carry):
            for i in range(width_x):
                here = work[step, c, i, lo:hi, :]
                west = xh[step, 0, c] if i == 0 else work[step, c, i - 1, lo:hi, :]
                east = xh[step, 1, c] if i == width_x - 1 else work[step, c, i + 1, lo:hi, :]
                south = work[step, c, i, lo - 1:hi - 1, :]
                north = work[step, c, i, lo + 1:hi + 1, :]
                target[c, i, lo:hi, :] = (
                    source[c, i]
                    + terms[0, i] * west
                    + terms[1, i] * east
                    + terms[2, i] * south
                    + terms[3, i] * north
                    + terms[4, i] * pltpu.roll(here, 1, 1)
                    + terms[5, i] * pltpu.roll(here, height - 1, 1)
                )
            return carry

        lax.fori_loop(0, 3, component, 0)
        if step + 1 < SWEEPS:
            sends = exchange(step + 1, target, lo, True)

    last = [
        send(out.at[:, :, pl.ds(lo, REACH), :], gh.at[1], gsem, 1, down),
        send(out.at[:, :, pl.ds(hi - REACH, REACH), :], gh.at[0], gsem, 0, up),
    ]
    for copy in last:
        copy.wait()
    out[:, :, 0:lo, :] = gh[0]
    out[:, :, hi:hi + REACH, :] = gh[1]


def fit(w, r, points):
    spread = jnp.sum(r[0] * r[0] + r[1] * r[1] + r[2] * r[2], axis=1, keepdims=True)
    mean = [jnp.sum(w[c], axis=1, keepdims=True) / points for c in range(3)]
    spin = []
    for c in range(3):
        a, b = (c + 1) % 3, (c + 2) % 3
        moment = jnp.sum(r[a] * w[b] - r[b] * w[a], axis=1, keepdims=True)
        spin.append(1.5 * moment / spread)
    return mean, spin


def update_kernel(sampled, radius, lam, out, near_left, near_right, far_left, far_right, sems):
    left, right, _, _ = around()
    count = lax.axis_size("gx")
    far_down = (lax.rem(left[0] + count - 1, count), left[1])
    far_up = (lax.rem(right[0] + 1, count), right[1])
    slots, points = radius.shape[1] // 3, radius.shape[2]
    greet((left, right, far_down, far_up))
    sends = [
        send(sampled.at[:, pl.ds(0, slots), :], far_right, sems, 3, far_down),
        send(sampled.at[:, pl.ds(2 * slots, slots), :], far_left, sems, 2, far_up),
        send(sampled.at[:, pl.ds(0, 2 * slots), :], near_right, sems, 1, left),
        send(sampled.at[:, pl.ds(slots, 2 * slots), :], near_left, sems, 0, right),
    ]
    r = [radius[c] for c in range(3)]
    for copy in sends:
        copy.wait()
    w = []
    for c in range(3):
        first = near_left[c, 0:slots, :] + far_left[c]
        middle = near_left[c, slots:2 * slots, :] + near_right[c, 0:slots, :]
        last = near_right[c, slots:2 * slots, :] + far_right[c]
        w.append(sampled[c] + jnp.concatenate([first, middle, last], 0))
    mean, spin = fit(w, r, points)
    for c in range(3):
        a, b = (c + 1) % 3, (c + 2) % 3
        target = mean[c] + (spin[a] * r[b] - spin[b] * r[a])
        out[c] = lam[c] + UZAWA_STEP * (target - w[c])


def motion_kernel(sampled, radius, motion, wh, sems):
    left, right, _, _ = around()
    slots, points = radius.shape[1] // 3, radius.shape[2]
    greet((left, right))
    sends = [
        send(sampled.at[:, pl.ds(0, slots), :], wh.at[1], sems, 1, left),
        send(sampled.at[:, pl.ds(2 * slots, slots), :], wh.at[0], sems, 0, right),
    ]
    r = [radius[c, slots:2 * slots, :] for c in range(3)]
    for copy in sends:
        copy.wait()
    w = [sampled[c, slots:2 * slots, :] + wh[0, c] + wh[1, c] for c in range(3)]
    mean, spin = fit(w, r, points)
    lane = lax.broadcasted_iota(jnp.int32, motion.shape, 1)
    row = jnp.zeros(motion.shape, F32)
    for c, value in enumerate(mean + spin):
        row = jnp.where(lane == c, value, row)
    motion[...] = row


def setup_kernel(
    nu, geometry, lam, terms, key, depth, radius, meta, lam_out, xh, ys, yh, gh, lh, sems
):
    left, right, down, up = around()
    width_x, width_y, height = nu.shape
    slots = geometry.shape[1]
    greet((left, right, down, up))
    ys[1] = nu[:, 0, :]
    ys[0] = nu[:, width_y - 1, :]
    sends = [
        send(ys.at[1], yh.at[1], sems, 0, down),
        send(ys.at[0], yh.at[0], sems, 1, up),
        send(nu.at[0], xh.at[1], sems, 2, left),
        send(nu.at[width_x - 1], xh.at[0], sems, 3, right),
        send(geometry, gh.at[1], sems, 4, left),
        send(geometry, gh.at[0], sems, 5, right),
        send(lam, lh.at[1], sems, 6, left),
        send(lam, lh.at[0], sems, 7, right),
    ]
    for copy in sends:
        copy.wait()
    z = lax.broadcasted_iota(jnp.int32, (width_y, height), 1)
    for i in range(width_x):
        here = nu[i]
        west = xh[0] if i == 0 else nu[i - 1]
        east = xh[1] if i == width_x - 1 else nu[i + 1]
        south = jnp.concatenate([yh[0, i:i + 1, :], here[:-1]], 0)
        north = jnp.concatenate([here[1:], yh[1, i:i + 1, :]], 0)
        below = jnp.where(z == 0, here, pltpu.roll(here, 1, 1))
        above = jnp.where(z == height - 1, here, pltpu.roll(here, height - 1, 1))
        k = [0.5 * (here + side) for side in (west, east, south, north)]
        k += [VERTICAL_WEIGHT * 0.5 * (here + side) for side in (below, above)]
        inverse = 1.0 / (MASS_TERM + k[0] + k[1] + k[2] + k[3] + k[4] + k[5])
        k[4] = jnp.where(z == 0, 0.0, k[4])
        k[5] = jnp.where(z == height - 1, 0.0, k[5])
        for f in range(6):
            terms[f, i] = k[f] * inverse
        terms[6, i] = inverse
    lane = lax.broadcasted_iota(jnp.int32, (slots, meta.shape[1]), 1)
    groups = (gh.at[0], geometry, gh.at[1])
    values = (lh.at[0], lam, lh.at[1])
    for g in range(3):
        part = groups[g]
        rows = slice(g * slots, (g + 1) * slots)
        local_x = part[0] + (g - 1) * width_x
        inside = (local_x >= 0) & (local_x < width_x)
        key[rows, :] = jnp.where(inside, local_x * WINDOW + part[1], -1)
        depth[rows, :] = part[2]
        active = jnp.max(jnp.where(inside, 1.0, 0.0), axis=1, keepdims=True).astype(jnp.int32)
        meta[rows, :] = jnp.where(lane == 0, part[3, :, 0:1], active)
        for c in range(3):
            radius[c, rows, :] = part[4 + c].astype(F32)
            lam_out[c, rows, :] = values[g][c]


def on_device(
    velocity, forcing, viscosity, multipliers, sphere_centres, sphere_offsets, sphere_count
):
    _, width_x, width_y, height = velocity.shape
    slots, points = multipliers.shape[2], multipliers.shape[4]
    live = jnp.arange(slots) < sphere_count[0, 0]
    centres = sphere_centres[0, 0]
    offsets = jnp.moveaxis(sphere_offsets[0, 0], 1, 0)
    base = (centres[:, 1] // 8) * 8
    own_x = jnp.where(live[:, None], centres[:, 0:1] + offsets[0], -8 * width_x)
    own_y = (centres[:, 1] - base)[:, None] + offsets[1] + REACH
    own_z = centres[:, 2:3] + offsets[2]
    geometry = jnp.stack(
        [own_x, own_y, own_z, jnp.broadcast_to(base[:, None], own_x.shape), *offsets]
    ).astype(jnp.int32)
    wide = (3, width_x, width_y + 2 * REACH, height)
    shape = jax.ShapeDtypeStruct
    limit = 48 * 1024 * 1024
    scatter = pl.pallas_call(
        scatter_kernel,
        name="spread_force",
        out_shape=shape(wide, F32),
        in_specs=[SM, VM, VM, VM],
        out_specs=VM,
        compiler_params=pltpu.CompilerParams(vmem_limit_bytes=limit),
    )
    gather = pl.pallas_call(
        gather_kernel,
        name="sample_flow",
        out_shape=shape((3, 3 * slots, points), F32),
        in_specs=[SM, VM, VM, VM],
        out_specs=VM,
        compiler_params=pltpu.CompilerParams(vmem_limit_bytes=limit),
    )
    def relax(ghosts):
        return pl.pallas_call(
            functools.partial(relax_kernel, ghosts),
            name="relax_ghosts" if ghosts else "relax_first",
            out_shape=shape(wide, F32),
            in_specs=[VM] * 4,
            out_specs=VM,
            scratch_shapes=[
                pltpu.VMEM((SWEEPS,) + wide, F32),
                pltpu.VMEM((3, width_x, width_y, height), F32),
                pltpu.VMEM((SWEEPS, 2, 3, width_y, height), F32),
                pltpu.VMEM((SWEEPS, 2, 3, width_x, height), F32),
                pltpu.VMEM((SWEEPS, 2, 3, width_x, height), F32),
                pltpu.VMEM((2, 3, width_x, REACH, height), F32),
                pltpu.VMEM((2, 3, width_x, REACH, height), F32),
                pltpu.SemaphoreType.DMA((SWEEPS, 2, 2)),
                pltpu.SemaphoreType.DMA((SWEEPS, 2, 2)),
                pltpu.SemaphoreType.DMA((2, 2)),
                pltpu.SemaphoreType.DMA((2, 2)),
            ],
            compiler_params=pltpu.CompilerParams(
                collective_id=4 if ghosts else 1, has_side_effects=True, vmem_limit_bytes=limit
            ),
        )

    update = pl.pallas_call(
        update_kernel,
        name="fit_update",
        out_shape=shape((3, 3 * slots, points), F32),
        in_specs=[VM] * 3,
        out_specs=VM,
        scratch_shapes=[
            pltpu.VMEM((3, 2 * slots, points), F32),
            pltpu.VMEM((3, 2 * slots, points), F32),
            pltpu.VMEM((3, slots, points), F32),
            pltpu.VMEM((3, slots, points), F32),
            pltpu.SemaphoreType.DMA((2, 4)),
        ],
        compiler_params=pltpu.CompilerParams(
            collective_id=2, has_side_effects=True, vmem_limit_bytes=limit
        ),
    )
    conclude = pl.pallas_call(
        motion_kernel,
        name="fit_motion",
        out_shape=shape((slots, 128), F32),
        in_specs=[VM] * 2,
        out_specs=VM,
        scratch_shapes=[
            pltpu.VMEM((2, 3, slots, points), F32),
            pltpu.SemaphoreType.DMA((2, 2)),
        ],
        compiler_params=pltpu.CompilerParams(
            collective_id=3, has_side_effects=True, vmem_limit_bytes=limit
        ),
    )

    prepare = pl.pallas_call(
        setup_kernel,
        name="prepare",
        out_shape=(
            shape((7, width_x, width_y, height), F32),
            shape((3 * slots, points), jnp.int32),
            shape((3 * slots, points), jnp.int32),
            shape((3, 3 * slots, points), F32),
            shape((3 * slots, 128), jnp.int32),
            shape((3, 3 * slots, points), F32),
        ),
        in_specs=[VM] * 3,
        out_specs=(VM,) * 6,
        scratch_shapes=[
            pltpu.VMEM((2, width_y, height), F32),
            pltpu.VMEM((2, width_x, height), F32),
            pltpu.VMEM((2, width_x, height), F32),
            pltpu.VMEM((2, 7, slots, points), jnp.int32),
            pltpu.VMEM((2, 3, slots, points), F32),
            pltpu.SemaphoreType.DMA((2, 8)),
        ],
        compiler_params=pltpu.CompilerParams(
            collective_id=5, has_side_effects=True, vmem_limit_bytes=limit
        ),
    )
    terms, key, depth, radius, meta, lam = prepare(
        viscosity, geometry, jnp.moveaxis(multipliers[0, 0], 1, 0)
    )
    field = velocity
    for round_index in range(UZ):
        force = scatter(meta, key, depth, lam)
        field = relax(round_index > 0)(field, forcing, force, terms)
        sampled = gather(meta, key, depth, field)
        if round_index + 1 < UZ:
            lam = update(sampled, radius, lam)
    motion = conclude(sampled, radius)
    return field[:, :, REACH:REACH + width_y, :], motion[:, :6][None, None]


def solution(mesh):
    placed = (
        P(None, "gx", "gy", None),
        P(None, "gx", "gy", None),
        P("gx", "gy", None),
        P("gx", "gy", None, None, None),
        P("gx", "gy", None, None),
        P("gx", "gy", None, None, None),
        P("gx", "gy"),
    )
    return jax.shard_map(
        on_device,
        mesh=mesh,
        in_specs=placed,
        out_specs=(P(None, "gx", "gy", None), P("gx", "gy", None, None)),
        check_vma=False,
    )
```

```python
import functools

import jax
import jax.numpy as jnp
from jax import lax
from jax.experimental import pallas as pl
from jax.experimental.pallas import tpu as pltpu
from jax.sharding import PartitionSpec as P

SWEEPS = 4
UZ = 3
REACH = 8
WINDOW = 24

MASS_TERM = 0.2
VERTICAL_WEIGHT = 0.25
UZAWA_STEP = 0.5

MESH = pl.DeviceIdType.MESH
VM = pl.BlockSpec(memory_space=pltpu.VMEM)
SM = pl.BlockSpec(memory_space=pltpu.SMEM)
F32 = jnp.float32
BF16 = jnp.bfloat16


def around():
    nx, ny = lax.axis_size("gx"), lax.axis_size("gy")
    me_x, me_y = lax.axis_index("gx"), lax.axis_index("gy")
    left = (lax.rem(me_x + nx - 1, nx), me_y)
    right = (lax.rem(me_x + 1, nx), me_y)
    down = (me_x, lax.rem(me_y + ny - 1, ny))
    up = (me_x, lax.rem(me_y + 1, ny))
    return left, right, down, up


def greet(devices):
    barrier = pltpu.get_barrier_semaphore()
    for device in devices:
        pl.semaphore_signal(barrier, inc=1, device_id=device, device_id_type=MESH)
    pl.semaphore_wait(barrier, len(devices))


def send(src, dst, sems, index, device):
    copy = pltpu.make_async_remote_copy(
        src_ref=src,
        dst_ref=dst,
        send_sem=sems.at[0, index],
        recv_sem=sems.at[1, index],
        device_id=device,
        device_id_type=MESH,
    )
    copy.start()
    return copy


def scatter_kernel(meta, key, depth, lam, out):
    width_x = out.shape[1]
    height = out.shape[3]
    rows = width_x * WINDOW
    slots, points = key.shape
    out[...] = jnp.zeros_like(out)

    def one(s, carry):
        @pl.when(meta[s, 1] > 0)
        def _():
            base = pl.multiple_of(meta[s, 0], 8)
            row_key = key[pl.ds(s, 1), :]
            row_z = depth[pl.ds(s, 1), :]
            mask = lax.broadcasted_iota(jnp.int32, (rows, points), 0) == row_key
            mask = jnp.where(mask, 1.0, 0.0).astype(BF16)
            at_z = lax.broadcasted_iota(jnp.int32, (height, points), 0) == row_z
            at_z = jnp.where(at_z, 1.0, 0.0).astype(BF16)
            high, low = [], []
            for c in range(3):
                value = lam[c, pl.ds(s, 1), :]
                top = value.astype(BF16)
                rest = (value - top.astype(F32)).astype(BF16)
                high.append(at_z * top)
                low.append(at_z * rest)
            dims = (((1,), (1,)), ((), ()))
            got = lax.dot_general(
                mask, jnp.concatenate(high, 0), dims, preferred_element_type=F32
            ) + lax.dot_general(
                mask, jnp.concatenate(low, 0), dims, preferred_element_type=F32
            )
            for c in range(3):
                part = got[:, c * height:(c + 1) * height].reshape(width_x, WINDOW, height)
                out[c, :, pl.ds(base, WINDOW), :] += part

        return carry

    lax.fori_loop(0, slots, one, 0)


def gather_kernel(meta, key, depth, field, out):
    width_x = field.shape[1]
    height = field.shape[3]
    rows = width_x * WINDOW
    slots, points = key.shape
    out[...] = jnp.zeros_like(out)

    def one(s, carry):
        @pl.when(meta[s, 1] > 0)
        def _():
            base = pl.multiple_of(meta[s, 0], 8)
            row_key = key[pl.ds(s, 1), :]
            row_z = depth[pl.ds(s, 1), :]
            mask = lax.broadcasted_iota(jnp.int32, (rows, points), 0) == row_key
            at_z = lax.broadcasted_iota(jnp.int32, (height, points), 0) == row_z
            at_z = jnp.where(at_z, 1.0, 0.0).astype(BF16)
            at_z = jnp.concatenate([at_z, at_z], 0)
            for c in range(3):
                value = field[c, :, pl.ds(base, WINDOW), :].reshape(rows, height)
                top = value.astype(BF16)
                rest = (value - top.astype(F32)).astype(BF16)
                got = jnp.dot(
                    jnp.concatenate([top, rest], 1), at_z, preferred_element_type=F32
                )
                out[c, pl.ds(s, 1), :] = jnp.sum(
                    jnp.where(mask, got, 0.0), axis=0, keepdims=True
                )

        return carry

    lax.fori_loop(0, slots, one, 0)


def relax_kernel(
    ghosts, flow, forcing, partial, terms, out, work, source, xh, ys, yh, ph, gh, xsem, ysem, psem, gsem
):
    left, right, down, up = around()
    width_x, width_y, height = forcing.shape[1:]
    lo, hi = REACH, REACH + width_y
    greet((left, right, down, up))
    share = [
        send(partial.at[:, :, pl.ds(0, REACH), :], ph.at[1], psem, 1, down),
        send(partial.at[:, :, pl.ds(hi, REACH), :], ph.at[0], psem, 0, up),
    ]

    def exchange(step, x_ref, first_row, along_y):
        rows = pl.ds(first_row, width_y)
        copies = []
        if along_y:
            for c in range(3):
                ys[step, 1, c] = x_ref[c, :, first_row, :]
                ys[step, 0, c] = x_ref[c, :, first_row + width_y - 1, :]
            copies = [
                send(ys.at[step, 1], yh.at[step, 1], ysem.at[step], 1, down),
                send(ys.at[step, 0], yh.at[step, 0], ysem.at[step], 0, up),
            ]
        return copies + [
            send(x_ref.at[:, 0, rows, :], xh.at[step, 1], xsem.at[step], 1, left),
            send(x_ref.at[:, width_x - 1, rows, :], xh.at[step, 0], xsem.at[step], 0, right),
        ]

    sends = exchange(0, flow, lo if ghosts else 0, not ghosts)
    if ghosts:
        work[0] = flow[...]
    else:
        work[0, :, :, lo:hi, :] = flow[...]
    source[...] = (forcing[...] + partial[:, :, lo:hi, :]) * terms[6][None]
    for copy in share:
        copy.wait()
    source[:, :, 0:REACH, :] += ph[0] * terms[6, :, 0:REACH, :][None]
    source[:, :, width_y - REACH:width_y, :] += ph[1] * terms[6, :, width_y - REACH:width_y, :][None]

    for step in range(SWEEPS):
        for copy in sends:
            copy.wait()
        for c in range(3 if step > 0 or not ghosts else 0):
            for i in range(width_x):
                work[step, c, i, lo - 1:lo, :] = yh[step, 0, c, i:i + 1, :]
                work[step, c, i, hi:hi + 1, :] = yh[step, 1, c, i:i + 1, :]
        target = work.at[step + 1] if step + 1 < SWEEPS else out

        def component(c, carry):
            for i in range(width_x):
                here = work[step, c, i, lo:hi, :]
                west = xh[step, 0, c] if i == 0 else work[step, c, i - 1, lo:hi, :]
                east = xh[step, 1, c] if i == width_x - 1 else work[step, c, i + 1, lo:hi, :]
                south = work[step, c, i, lo - 1:hi - 1, :]
                north = work[step, c, i, lo + 1:hi + 1, :]
                target[c, i, lo:hi, :] = (
                    source[c, i]
                    + terms[0, i] * west
                    + terms[1, i] * east
                    + terms[2, i] * south
                    + terms[3, i] * north
                    + terms[4, i] * pltpu.roll(here, 1, 1)
                    + terms[5, i] * pltpu.roll(here, height - 1, 1)
                )
            return carry

        lax.fori_loop(0, 3, component, 0)
        if step + 1 < SWEEPS:
            sends = exchange(step + 1, target, lo, True)

    last = [
        send(out.at[:, :, pl.ds(lo, REACH), :], gh.at[1], gsem, 1, down),
        send(out.at[:, :, pl.ds(hi - REACH, REACH), :], gh.at[0], gsem, 0, up),
    ]
    for copy in last:
        copy.wait()
    out[:, :, 0:lo, :] = gh[0]
    out[:, :, hi:hi + REACH, :] = gh[1]


def fit(w, r, points):
    spread = jnp.sum(r[0] * r[0] + r[1] * r[1] + r[2] * r[2], axis=1, keepdims=True)
    mean = [jnp.sum(w[c], axis=1, keepdims=True) / points for c in range(3)]
    spin = []
    for c in range(3):
        a, b = (c + 1) % 3, (c + 2) % 3
        moment = jnp.sum(r[a] * w[b] - r[b] * w[a], axis=1, keepdims=True)
        spin.append(1.5 * moment / spread)
    return mean, spin


def update_kernel(sampled, radius, lam, out, near_left, near_right, far_left, far_right, sems):
    left, right, _, _ = around()
    count = lax.axis_size("gx")
    far_down = (lax.rem(left[0] + count - 1, count), left[1])
    far_up = (lax.rem(right[0] + 1, count), right[1])
    slots, points = radius.shape[1] // 3, radius.shape[2]
    greet((left, right, far_down, far_up))
    sends = [
        send(sampled.at[:, pl.ds(0, slots), :], far_right, sems, 3, far_down),
        send(sampled.at[:, pl.ds(2 * slots, slots), :], far_left, sems, 2, far_up),
        send(sampled.at[:, pl.ds(0, 2 * slots), :], near_right, sems, 1, left),
        send(sampled.at[:, pl.ds(slots, 2 * slots), :], near_left, sems, 0, right),
    ]
    r = [radius[c] for c in range(3)]
    for copy in sends:
        copy.wait()
    w = []
    for c in range(3):
        first = near_left[c, 0:slots, :] + far_left[c]
        middle = near_left[c, slots:2 * slots, :] + near_right[c, 0:slots, :]
        last = near_right[c, slots:2 * slots, :] + far_right[c]
        w.append(sampled[c] + jnp.concatenate([first, middle, last], 0))
    mean, spin = fit(w, r, points)
    for c in range(3):
        a, b = (c + 1) % 3, (c + 2) % 3
        target = mean[c] + (spin[a] * r[b] - spin[b] * r[a])
        out[c] = lam[c] + UZAWA_STEP * (target - w[c])


def motion_kernel(sampled, radius, motion, wh, sems):
    left, right, _, _ = around()
    slots, points = radius.shape[1] // 3, radius.shape[2]
    greet((left, right))
    sends = [
        send(sampled.at[:, pl.ds(0, slots), :], wh.at[1], sems, 1, left),
        send(sampled.at[:, pl.ds(2 * slots, slots), :], wh.at[0], sems, 0, right),
    ]
    r = [radius[c, slots:2 * slots, :] for c in range(3)]
    for copy in sends:
        copy.wait()
    w = [sampled[c, slots:2 * slots, :] + wh[0, c] + wh[1, c] for c in range(3)]
    mean, spin = fit(w, r, points)
    lane = lax.broadcasted_iota(jnp.int32, motion.shape, 1)
    row = jnp.zeros(motion.shape, F32)
    for c, value in enumerate(mean + spin):
        row = jnp.where(lane == c, value, row)
    motion[...] = row


def setup_kernel(
    nu, geometry, lam, terms, key, depth, radius, meta, lam_out, xh, ys, yh, gh, lh, sems
):
    left, right, down, up = around()
    width_x, width_y, height = nu.shape
    slots = geometry.shape[1]
    greet((left, right, down, up))
    ys[1] = nu[:, 0, :]
    ys[0] = nu[:, width_y - 1, :]
    sends = [
        send(ys.at[1], yh.at[1], sems, 0, down),
        send(ys.at[0], yh.at[0], sems, 1, up),
        send(nu.at[0], xh.at[1], sems, 2, left),
        send(nu.at[width_x - 1], xh.at[0], sems, 3, right),
        send(geometry, gh.at[1], sems, 4, left),
        send(geometry, gh.at[0], sems, 5, right),
        send(lam, lh.at[1], sems, 6, left),
        send(lam, lh.at[0], sems, 7, right),
    ]
    for copy in sends:
        copy.wait()
    z = lax.broadcasted_iota(jnp.int32, (width_y, height), 1)
    for i in range(width_x):
        here = nu[i]
        west = xh[0] if i == 0 else nu[i - 1]
        east = xh[1] if i == width_x - 1 else nu[i + 1]
        south = jnp.concatenate([yh[0, i:i + 1, :], here[:-1]], 0)
        north = jnp.concatenate([here[1:], yh[1, i:i + 1, :]], 0)
        below = jnp.where(z == 0, here, pltpu.roll(here, 1, 1))
        above = jnp.where(z == height - 1, here, pltpu.roll(here, height - 1, 1))
        k = [0.5 * (here + side) for side in (west, east, south, north)]
        k += [VERTICAL_WEIGHT * 0.5 * (here + side) for side in (below, above)]
        inverse = 1.0 / (MASS_TERM + k[0] + k[1] + k[2] + k[3] + k[4] + k[5])
        k[4] = jnp.where(z == 0, 0.0, k[4])
        k[5] = jnp.where(z == height - 1, 0.0, k[5])
        for f in range(6):
            terms[f, i] = k[f] * inverse
        terms[6, i] = inverse
    lane = lax.broadcasted_iota(jnp.int32, (slots, meta.shape[1]), 1)
    groups = (gh.at[0], geometry, gh.at[1])
    values = (lh.at[0], lam, lh.at[1])
    for g in range(3):
        part = groups[g]
        rows = slice(g * slots, (g + 1) * slots)
        local_x = part[0] + (g - 1) * width_x
        inside = (local_x >= 0) & (local_x < width_x)
        key[rows, :] = jnp.where(inside, local_x * WINDOW + part[1], -1)
        depth[rows, :] = part[2]
        active = jnp.max(jnp.where(inside, 1.0, 0.0), axis=1, keepdims=True).astype(jnp.int32)
        meta[rows, :] = jnp.where(lane == 0, part[3, :, 0:1], active)
        for c in range(3):
            radius[c, rows, :] = part[4 + c].astype(F32)
            lam_out[c, rows, :] = values[g][c]


def on_device(
    velocity, forcing, viscosity, multipliers, sphere_centres, sphere_offsets, sphere_count
):
    _, width_x, width_y, height = velocity.shape
    slots, points = multipliers.shape[2], multipliers.shape[4]
    live = jnp.arange(slots) < sphere_count[0, 0]
    centres = sphere_centres[0, 0]
    offsets = jnp.moveaxis(sphere_offsets[0, 0], 1, 0)
    base = (centres[:, 1] // 8) * 8
    own_x = jnp.where(live[:, None], centres[:, 0:1] + offsets[0], -8 * width_x)
    own_y = (centres[:, 1] - base)[:, None] + offsets[1] + REACH
    own_z = centres[:, 2:3] + offsets[2]
    geometry = jnp.stack(
        [own_x, own_y, own_z, jnp.broadcast_to(base[:, None], own_x.shape), *offsets]
    ).astype(jnp.int32)
    wide = (3, width_x, width_y + 2 * REACH, height)
    shape = jax.ShapeDtypeStruct
    limit = 48 * 1024 * 1024
    scatter = pl.pallas_call(
        scatter_kernel,
        name="spread_force",
        out_shape=shape(wide, F32),
        in_specs=[SM, VM, VM, VM],
        out_specs=VM,
        compiler_params=pltpu.CompilerParams(vmem_limit_bytes=limit),
    )
    gather = pl.pallas_call(
        gather_kernel,
        name="sample_flow",
        out_shape=shape((3, 3 * slots, points), F32),
        in_specs=[SM, VM, VM, VM],
        out_specs=VM,
        compiler_params=pltpu.CompilerParams(vmem_limit_bytes=limit),
    )
    def relax(ghosts):
        return pl.pallas_call(
            functools.partial(relax_kernel, ghosts),
            name="relax_ghosts" if ghosts else "relax_first",
            out_shape=shape(wide, F32),
            in_specs=[VM] * 4,
            out_specs=VM,
            scratch_shapes=[
                pltpu.VMEM((SWEEPS,) + wide, F32),
                pltpu.VMEM((3, width_x, width_y, height), F32),
                pltpu.VMEM((SWEEPS, 2, 3, width_y, height), F32),
                pltpu.VMEM((SWEEPS, 2, 3, width_x, height), F32),
                pltpu.VMEM((SWEEPS, 2, 3, width_x, height), F32),
                pltpu.VMEM((2, 3, width_x, REACH, height), F32),
                pltpu.VMEM((2, 3, width_x, REACH, height), F32),
                pltpu.SemaphoreType.DMA((SWEEPS, 2, 2)),
                pltpu.SemaphoreType.DMA((SWEEPS, 2, 2)),
                pltpu.SemaphoreType.DMA((2, 2)),
                pltpu.SemaphoreType.DMA((2, 2)),
            ],
            compiler_params=pltpu.CompilerParams(
                collective_id=4 if ghosts else 1, has_side_effects=True, vmem_limit_bytes=limit
            ),
        )

    update = pl.pallas_call(
        update_kernel,
        name="fit_update",
        out_shape=shape((3, 3 * slots, points), F32),
        in_specs=[VM] * 3,
        out_specs=VM,
        scratch_shapes=[
            pltpu.VMEM((3, 2 * slots, points), F32),
            pltpu.VMEM((3, 2 * slots, points), F32),
            pltpu.VMEM((3, slots, points), F32),
            pltpu.VMEM((3, slots, points), F32),
            pltpu.SemaphoreType.DMA((2, 4)),
        ],
        compiler_params=pltpu.CompilerParams(
            collective_id=2, has_side_effects=True, vmem_limit_bytes=limit
        ),
    )
    conclude = pl.pallas_call(
        motion_kernel,
        name="fit_motion",
        out_shape=shape((slots, 128), F32),
        in_specs=[VM] * 2,
        out_specs=VM,
        scratch_shapes=[
            pltpu.VMEM((2, 3, slots, points), F32),
            pltpu.SemaphoreType.DMA((2, 2)),
        ],
        compiler_params=pltpu.CompilerParams(
            collective_id=3, has_side_effects=True, vmem_limit_bytes=limit
        ),
    )

    prepare = pl.pallas_call(
        setup_kernel,
        name="prepare",
        out_shape=(
            shape((7, width_x, width_y, height), F32),
            shape((3 * slots, points), jnp.int32),
            shape((3 * slots, points), jnp.int32),
            shape((3, 3 * slots, points), F32),
            shape((3 * slots, 128), jnp.int32),
            shape((3, 3 * slots, points), F32),
        ),
        in_specs=[VM] * 3,
        out_specs=(VM,) * 6,
        scratch_shapes=[
            pltpu.VMEM((2, width_y, height), F32),
            pltpu.VMEM((2, width_x, height), F32),
            pltpu.VMEM((2, width_x, height), F32),
            pltpu.VMEM((2, 7, slots, points), jnp.int32),
            pltpu.VMEM((2, 3, slots, points), F32),
            pltpu.SemaphoreType.DMA((2, 8)),
        ],
        compiler_params=pltpu.CompilerParams(
            collective_id=5, has_side_effects=True, vmem_limit_bytes=limit
        ),
    )
    terms, key, depth, radius, meta, lam = prepare(
        viscosity, geometry, jnp.moveaxis(multipliers[0, 0], 1, 0)
    )
    field = velocity
    for round_index in range(UZ):
        force = scatter(meta, key, depth, lam)
        field = relax(round_index > 0)(field, forcing, force, terms)
        sampled = gather(meta, key, depth, field)
        if round_index + 1 < UZ:
            lam = update(sampled, radius, lam)
    motion = conclude(sampled, radius)
    return field[:, :, REACH:REACH + width_y, :], motion[:, :6][None, None]


def solution(mesh):
    placed = (
        P(None, "gx", "gy", None),
        P(None, "gx", "gy", None),
        P("gx", "gy", None),
        P("gx", "gy", None, None, None),
        P("gx", "gy", None, None),
        P("gx", "gy", None, None, None),
        P("gx", "gy"),
    )
    return jax.shard_map(
        on_device,
        mesh=mesh,
        in_specs=placed,
        out_specs=(P(None, "gx", "gy", None), P("gx", "gy", None, None)),
        check_vma=False,
    )
```

```python
import functools

import jax
import jax.numpy as jnp
from jax import lax
from jax.experimental import pallas as pl
from jax.experimental.pallas import tpu as pltpu
from jax.sharding import PartitionSpec as P

SWEEPS = 4
UZ = 3
REACH = 8
WINDOW = 24

MASS_TERM = 0.2
VERTICAL_WEIGHT = 0.25
UZAWA_STEP = 0.5

MESH = pl.DeviceIdType.MESH
VM = pl.BlockSpec(memory_space=pltpu.VMEM)
SM = pl.BlockSpec(memory_space=pltpu.SMEM)
F32 = jnp.float32
BF16 = jnp.bfloat16


def around():
    nx, ny = lax.axis_size("gx"), lax.axis_size("gy")
    me_x, me_y = lax.axis_index("gx"), lax.axis_index("gy")
    left = (lax.rem(me_x + nx - 1, nx), me_y)
    right = (lax.rem(me_x + 1, nx), me_y)
    down = (me_x, lax.rem(me_y + ny - 1, ny))
    up = (me_x, lax.rem(me_y + 1, ny))
    return left, right, down, up


def greet(devices):
    barrier = pltpu.get_barrier_semaphore()
    for device in devices:
        pl.semaphore_signal(barrier, inc=1, device_id=device, device_id_type=MESH)
    pl.semaphore_wait(barrier, len(devices))


def send(src, dst, sems, index, device):
    copy = pltpu.make_async_remote_copy(
        src_ref=src,
        dst_ref=dst,
        send_sem=sems.at[0, index],
        recv_sem=sems.at[1, index],
        device_id=device,
        device_id_type=MESH,
    )
    copy.start()
    return copy


def scatter_kernel(meta, key, depth, lam, out):
    width_x = out.shape[1]
    height = out.shape[3]
    rows = width_x * WINDOW
    slots, points = key.shape
    out[...] = jnp.zeros_like(out)

    def one(s, carry):
        @pl.when(meta[s, 1] > 0)
        def _():
            base = pl.multiple_of(meta[s, 0], 8)
            row_key = key[pl.ds(s, 1), :]
            row_z = depth[pl.ds(s, 1), :]
            mask = lax.broadcasted_iota(jnp.int32, (rows, points), 0) == row_key
            mask = jnp.where(mask, 1.0, 0.0).astype(BF16)
            at_z = lax.broadcasted_iota(jnp.int32, (height, points), 0) == row_z
            at_z = jnp.where(at_z, 1.0, 0.0).astype(BF16)
            high, low = [], []
            for c in range(3):
                value = lam[c, pl.ds(s, 1), :]
                top = value.astype(BF16)
                rest = (value - top.astype(F32)).astype(BF16)
                high.append(at_z * top)
                low.append(at_z * rest)
            dims = (((1,), (1,)), ((), ()))
            got = lax.dot_general(
                mask, jnp.concatenate(high, 0), dims, preferred_element_type=F32
            ) + lax.dot_general(
                mask, jnp.concatenate(low, 0), dims, preferred_element_type=F32
            )
            for c in range(3):
                part = got[:, c * height:(c + 1) * height].reshape(width_x, WINDOW, height)
                out[c, :, pl.ds(base, WINDOW), :] += part

        return carry

    lax.fori_loop(0, slots, one, 0)


def gather_kernel(meta, key, depth, field, out):
    width_x = field.shape[1]
    height = field.shape[3]
    rows = width_x * WINDOW
    slots, points = key.shape
    out[...] = jnp.zeros_like(out)

    def one(s, carry):
        @pl.when(meta[s, 1] > 0)
        def _():
            base = pl.multiple_of(meta[s, 0], 8)
            row_key = key[pl.ds(s, 1), :]
            row_z = depth[pl.ds(s, 1), :]
            mask = lax.broadcasted_iota(jnp.int32, (rows, points), 0) == row_key
            at_z = lax.broadcasted_iota(jnp.int32, (height, points), 0) == row_z
            at_z = jnp.where(at_z, 1.0, 0.0).astype(BF16)
            at_z = jnp.concatenate([at_z, at_z], 0)
            value = field[:, :, pl.ds(base, WINDOW), :].reshape(3 * rows, height)
            top = value.astype(BF16)
            rest = (value - top.astype(F32)).astype(BF16)
            got = jnp.dot(
                jnp.concatenate([top, rest], 1), at_z, preferred_element_type=F32
            )
            for c in range(3):
                out[c, pl.ds(s, 1), :] = jnp.sum(
                    jnp.where(mask, got[c * rows:(c + 1) * rows], 0.0), axis=0, keepdims=True
                )

        return carry

    lax.fori_loop(0, slots, one, 0)


def relax_kernel(
    ghosts, flow, forcing, partial, terms, out, work, source, xh, ys, yh, ph, gh, xsem, ysem, psem, gsem
):
    left, right, down, up = around()
    width_x, width_y, height = forcing.shape[1:]
    lo, hi = REACH, REACH + width_y
    greet((left, right, down, up))
    share = [
        send(partial.at[:, :, pl.ds(0, REACH), :], ph.at[1], psem, 1, down),
        send(partial.at[:, :, pl.ds(hi, REACH), :], ph.at[0], psem, 0, up),
    ]

    def exchange(step, x_ref, first_row, along_y):
        rows = pl.ds(first_row, width_y)
        copies = []
        if along_y:
            for c in range(3):
                ys[step, 1, c] = x_ref[c, :, first_row, :]
                ys[step, 0, c] = x_ref[c, :, first_row + width_y - 1, :]
            copies = [
                send(ys.at[step, 1], yh.at[step, 1], ysem.at[step], 1, down),
                send(ys.at[step, 0], yh.at[step, 0], ysem.at[step], 0, up),
            ]
        return copies + [
            send(x_ref.at[:, 0, rows, :], xh.at[step, 1], xsem.at[step], 1, left),
            send(x_ref.at[:, width_x - 1, rows, :], xh.at[step, 0], xsem.at[step], 0, right),
        ]

    sends = exchange(0, flow, lo if ghosts else 0, not ghosts)
    if ghosts:
        work[0] = flow[...]
    else:
        work[0, :, :, lo:hi, :] = flow[...]
    source[...] = (forcing[...] + partial[:, :, lo:hi, :]) * terms[6][None]
    for copy in share:
        copy.wait()
    source[:, :, 0:REACH, :] += ph[0] * terms[6, :, 0:REACH, :][None]
    source[:, :, width_y - REACH:width_y, :] += ph[1] * terms[6, :, width_y - REACH:width_y, :][None]

    for step in range(SWEEPS):
        for copy in sends:
            copy.wait()
        for c in range(3 if step > 0 or not ghosts else 0):
            for i in range(width_x):
                work[step, c, i, lo - 1:lo, :] = yh[step, 0, c, i:i + 1, :]
                work[step, c, i, hi:hi + 1, :] = yh[step, 1, c, i:i + 1, :]
        target = work.at[step + 1] if step + 1 < SWEEPS else out

        def component(c, carry):
            for i in range(width_x):
                here = work[step, c, i, lo:hi, :]
                west = xh[step, 0, c] if i == 0 else work[step, c, i - 1, lo:hi, :]
                east = xh[step, 1, c] if i == width_x - 1 else work[step, c, i + 1, lo:hi, :]
                south = work[step, c, i, lo - 1:hi - 1, :]
                north = work[step, c, i, lo + 1:hi + 1, :]
                target[c, i, lo:hi, :] = (
                    source[c, i]
                    + terms[0, i] * west
                    + terms[1, i] * east
                    + terms[2, i] * south
                    + terms[3, i] * north
                    + terms[4, i] * pltpu.roll(here, 1, 1)
                    + terms[5, i] * pltpu.roll(here, height - 1, 1)
                )
            return carry

        lax.fori_loop(0, 3, component, 0)
        if step + 1 < SWEEPS:
            sends = exchange(step + 1, target, lo, True)

    last = [
        send(out.at[:, :, pl.ds(lo, REACH), :], gh.at[1], gsem, 1, down),
        send(out.at[:, :, pl.ds(hi - REACH, REACH), :], gh.at[0], gsem, 0, up),
    ]
    for copy in last:
        copy.wait()
    out[:, :, 0:lo, :] = gh[0]
    out[:, :, hi:hi + REACH, :] = gh[1]


def fit(w, r, points):
    spread = jnp.sum(r[0] * r[0] + r[1] * r[1] + r[2] * r[2], axis=1, keepdims=True)
    mean = [jnp.sum(w[c], axis=1, keepdims=True) / points for c in range(3)]
    spin = []
    for c in range(3):
        a, b = (c + 1) % 3, (c + 2) % 3
        moment = jnp.sum(r[a] * w[b] - r[b] * w[a], axis=1, keepdims=True)
        spin.append(1.5 * moment / spread)
    return mean, spin


def update_kernel(sampled, radius, lam, out, near_left, near_right, far_left, far_right, sems):
    left, right, _, _ = around()
    count = lax.axis_size("gx")
    far_down = (lax.rem(left[0] + count - 1, count), left[1])
    far_up = (lax.rem(right[0] + 1, count), right[1])
    slots, points = radius.shape[1] // 3, radius.shape[2]
    greet((left, right, far_down, far_up))
    sends = [
        send(sampled.at[:, pl.ds(0, slots), :], far_right, sems, 3, far_down),
        send(sampled.at[:, pl.ds(2 * slots, slots), :], far_left, sems, 2, far_up),
        send(sampled.at[:, pl.ds(0, 2 * slots), :], near_right, sems, 1, left),
        send(sampled.at[:, pl.ds(slots, 2 * slots), :], near_left, sems, 0, right),
    ]
    r = [radius[c] for c in range(3)]
    for copy in sends:
        copy.wait()
    w = []
    for c in range(3):
        first = near_left[c, 0:slots, :] + far_left[c]
        middle = near_left[c, slots:2 * slots, :] + near_right[c, 0:slots, :]
        last = near_right[c, slots:2 * slots, :] + far_right[c]
        w.append(sampled[c] + jnp.concatenate([first, middle, last], 0))
    mean, spin = fit(w, r, points)
    for c in range(3):
        a, b = (c + 1) % 3, (c + 2) % 3
        target = mean[c] + (spin[a] * r[b] - spin[b] * r[a])
        out[c] = lam[c] + UZAWA_STEP * (target - w[c])


def motion_kernel(sampled, radius, motion, wh, sems):
    left, right, _, _ = around()
    slots, points = radius.shape[1] // 3, radius.shape[2]
    greet((left, right))
    sends = [
        send(sampled.at[:, pl.ds(0, slots), :], wh.at[1], sems, 1, left),
        send(sampled.at[:, pl.ds(2 * slots, slots), :], wh.at[0], sems, 0, right),
    ]
    r = [radius[c, slots:2 * slots, :] for c in range(3)]
    for copy in sends:
        copy.wait()
    w = [sampled[c, slots:2 * slots, :] + wh[0, c] + wh[1, c] for c in range(3)]
    mean, spin = fit(w, r, points)
    lane = lax.broadcasted_iota(jnp.int32, motion.shape, 1)
    row = jnp.zeros(motion.shape, F32)
    for c, value in enumerate(mean + spin):
        row = jnp.where(lane == c, value, row)
    motion[...] = row


def setup_kernel(
    nu, geometry, lam, terms, key, depth, radius, meta, lam_out, xh, ys, yh, gh, lh, sems
):
    left, right, down, up = around()
    width_x, width_y, height = nu.shape
    slots = geometry.shape[1]
    greet((left, right, down, up))
    ys[1] = nu[:, 0, :]
    ys[0] = nu[:, width_y - 1, :]
    sends = [
        send(ys.at[1], yh.at[1], sems, 0, down),
        send(ys.at[0], yh.at[0], sems, 1, up),
        send(nu.at[0], xh.at[1], sems, 2, left),
        send(nu.at[width_x - 1], xh.at[0], sems, 3, right),
        send(geometry, gh.at[1], sems, 4, left),
        send(geometry, gh.at[0], sems, 5, right),
        send(lam, lh.at[1], sems, 6, left),
        send(lam, lh.at[0], sems, 7, right),
    ]
    for copy in sends:
        copy.wait()
    z = lax.broadcasted_iota(jnp.int32, (width_y, height), 1)
    for i in range(width_x):
        here = nu[i]
        west = xh[0] if i == 0 else nu[i - 1]
        east = xh[1] if i == width_x - 1 else nu[i + 1]
        south = jnp.concatenate([yh[0, i:i + 1, :], here[:-1]], 0)
        north = jnp.concatenate([here[1:], yh[1, i:i + 1, :]], 0)
        below = jnp.where(z == 0, here, pltpu.roll(here, 1, 1))
        above = jnp.where(z == height - 1, here, pltpu.roll(here, height - 1, 1))
        k = [0.5 * (here + side) for side in (west, east, south, north)]
        k += [VERTICAL_WEIGHT * 0.5 * (here + side) for side in (below, above)]
        inverse = 1.0 / (MASS_TERM + k[0] + k[1] + k[2] + k[3] + k[4] + k[5])
        k[4] = jnp.where(z == 0, 0.0, k[4])
        k[5] = jnp.where(z == height - 1, 0.0, k[5])
        for f in range(6):
            terms[f, i] = k[f] * inverse
        terms[6, i] = inverse
    lane = lax.broadcasted_iota(jnp.int32, (slots, meta.shape[1]), 1)
    groups = (gh.at[0], geometry, gh.at[1])
    values = (lh.at[0], lam, lh.at[1])
    for g in range(3):
        part = groups[g]
        rows = slice(g * slots, (g + 1) * slots)
        local_x = part[0] + (g - 1) * width_x
        inside = (local_x >= 0) & (local_x < width_x)
        key[rows, :] = jnp.where(inside, local_x * WINDOW + part[1], -1)
        depth[rows, :] = part[2]
        active = jnp.max(jnp.where(inside, 1.0, 0.0), axis=1, keepdims=True).astype(jnp.int32)
        meta[rows, :] = jnp.where(lane == 0, part[3, :, 0:1], active)
        for c in range(3):
            radius[c, rows, :] = part[4 + c].astype(F32)
            lam_out[c, rows, :] = values[g][c]


def on_device(
    velocity, forcing, viscosity, multipliers, sphere_centres, sphere_offsets, sphere_count
):
    _, width_x, width_y, height = velocity.shape
    slots, points = multipliers.shape[2], multipliers.shape[4]
    live = jnp.arange(slots) < sphere_count[0, 0]
    centres = sphere_centres[0, 0]
    offsets = jnp.moveaxis(sphere_offsets[0, 0], 1, 0)
    base = (centres[:, 1] // 8) * 8
    own_x = jnp.where(live[:, None], centres[:, 0:1] + offsets[0], -8 * width_x)
    own_y = (centres[:, 1] - base)[:, None] + offsets[1] + REACH
    own_z = centres[:, 2:3] + offsets[2]
    geometry = jnp.stack(
        [own_x, own_y, own_z, jnp.broadcast_to(base[:, None], own_x.shape), *offsets]
    ).astype(jnp.int32)
    wide = (3, width_x, width_y + 2 * REACH, height)
    shape = jax.ShapeDtypeStruct
    limit = 48 * 1024 * 1024
    scatter = pl.pallas_call(
        scatter_kernel,
        name="spread_force",
        out_shape=shape(wide, F32),
        in_specs=[SM, VM, VM, VM],
        out_specs=VM,
        compiler_params=pltpu.CompilerParams(vmem_limit_bytes=limit),
    )
    gather = pl.pallas_call(
        gather_kernel,
        name="sample_flow",
        out_shape=shape((3, 3 * slots, points), F32),
        in_specs=[SM, VM, VM, VM],
        out_specs=VM,
        compiler_params=pltpu.CompilerParams(vmem_limit_bytes=limit),
    )
    def relax(ghosts):
        return pl.pallas_call(
            functools.partial(relax_kernel, ghosts),
            name="relax_ghosts" if ghosts else "relax_first",
            out_shape=shape(wide, F32),
            in_specs=[VM] * 4,
            out_specs=VM,
            scratch_shapes=[
                pltpu.VMEM((SWEEPS,) + wide, F32),
                pltpu.VMEM((3, width_x, width_y, height), F32),
                pltpu.VMEM((SWEEPS, 2, 3, width_y, height), F32),
                pltpu.VMEM((SWEEPS, 2, 3, width_x, height), F32),
                pltpu.VMEM((SWEEPS, 2, 3, width_x, height), F32),
                pltpu.VMEM((2, 3, width_x, REACH, height), F32),
                pltpu.VMEM((2, 3, width_x, REACH, height), F32),
                pltpu.SemaphoreType.DMA((SWEEPS, 2, 2)),
                pltpu.SemaphoreType.DMA((SWEEPS, 2, 2)),
                pltpu.SemaphoreType.DMA((2, 2)),
                pltpu.SemaphoreType.DMA((2, 2)),
            ],
            compiler_params=pltpu.CompilerParams(
                collective_id=4 if ghosts else 1, has_side_effects=True, vmem_limit_bytes=limit
            ),
        )

    update = pl.pallas_call(
        update_kernel,
        name="fit_update",
        out_shape=shape((3, 3 * slots, points), F32),
        in_specs=[VM] * 3,
        out_specs=VM,
        scratch_shapes=[
            pltpu.VMEM((3, 2 * slots, points), F32),
            pltpu.VMEM((3, 2 * slots, points), F32),
            pltpu.VMEM((3, slots, points), F32),
            pltpu.VMEM((3, slots, points), F32),
            pltpu.SemaphoreType.DMA((2, 4)),
        ],
        compiler_params=pltpu.CompilerParams(
            collective_id=2, has_side_effects=True, vmem_limit_bytes=limit
        ),
    )
    conclude = pl.pallas_call(
        motion_kernel,
        name="fit_motion",
        out_shape=shape((slots, 128), F32),
        in_specs=[VM] * 2,
        out_specs=VM,
        scratch_shapes=[
            pltpu.VMEM((2, 3, slots, points), F32),
            pltpu.SemaphoreType.DMA((2, 2)),
        ],
        compiler_params=pltpu.CompilerParams(
            collective_id=3, has_side_effects=True, vmem_limit_bytes=limit
        ),
    )

    prepare = pl.pallas_call(
        setup_kernel,
        name="prepare",
        out_shape=(
            shape((7, width_x, width_y, height), F32),
            shape((3 * slots, points), jnp.int32),
            shape((3 * slots, points), jnp.int32),
            shape((3, 3 * slots, points), F32),
            shape((3 * slots, 128), jnp.int32),
            shape((3, 3 * slots, points), F32),
        ),
        in_specs=[VM] * 3,
        out_specs=(VM,) * 6,
        scratch_shapes=[
            pltpu.VMEM((2, width_y, height), F32),
            pltpu.VMEM((2, width_x, height), F32),
            pltpu.VMEM((2, width_x, height), F32),
            pltpu.VMEM((2, 7, slots, points), jnp.int32),
            pltpu.VMEM((2, 3, slots, points), F32),
            pltpu.SemaphoreType.DMA((2, 8)),
        ],
        compiler_params=pltpu.CompilerParams(
            collective_id=5, has_side_effects=True, vmem_limit_bytes=limit
        ),
    )
    terms, key, depth, radius, meta, lam = prepare(
        viscosity, geometry, jnp.moveaxis(multipliers[0, 0], 1, 0)
    )
    field = velocity
    for round_index in range(UZ):
        force = scatter(meta, key, depth, lam)
        field = relax(round_index > 0)(field, forcing, force, terms)
        sampled = gather(meta, key, depth, field)
        if round_index + 1 < UZ:
            lam = update(sampled, radius, lam)
    motion = conclude(sampled, radius)
    return field[:, :, REACH:REACH + width_y, :], motion[:, :6][None, None]


def solution(mesh):
    placed = (
        P(None, "gx", "gy", None),
        P(None, "gx", "gy", None),
        P("gx", "gy", None),
        P("gx", "gy", None, None, None),
        P("gx", "gy", None, None),
        P("gx", "gy", None, None, None),
        P("gx", "gy"),
    )
    return jax.shard_map(
        on_device,
        mesh=mesh,
        in_specs=placed,
        out_specs=(P(None, "gx", "gy", None), P("gx", "gy", None, None)),
        check_vma=False,
    )
```
